32 devices in a mesh: grp: 2 (over x), pool: 4 (over y, core), tp: 4 (over z).
Axes of the slice: x: 2, y: 2, z: 4, core: 2. Of those that a mesh axis runs over, the one named last changes fastest.
Arguments:
- queries: bfloat16 [3, 16, 6144], P(None, ('grp', 'pool'), 'tp'), parts along dimension 1, may hold values from -23 to 23
- new_kv: bfloat16 [3, 16, 2, 1024], P(None, ('grp', 'pool'), None, 'tp'), parts along dimension 1, may hold values from -5 to 5
- kv_cache: bfloat16 [3, 16, 2, 256, 1024], P(None, ('grp', 'pool'), None, None, 'tp'), parts along dimension 1, may hold values from -5 to 5
- cache_lengths: int32 [3, 16], P(None, ('grp', 'pool')), parts along dimension 1, may hold values from 1 to 256, 1024 in all within a row
- residual_in: bfloat16 [3, 16, 6144], P(None, 'grp', ('pool', 'tp')), parts along dimension 1, may hold values from -6 to 6
- out_weight: bfloat16 [6144, 6144], P('tp', 'pool'), may hold values from -0.625 to 0.625
- norm_gain: bfloat16 [6144], replicated, may hold values from 0.099609375 to 1.8984375
- router_weight: bfloat16 [6144, 4], replicated, may hold values from -0.078125 to 0.078125
- expert_in: bfloat16 [4, 2, 6144, 8192], P('pool', None, None, 'tp'), may hold values from -0.078125 to 0.078125
- expert_out: bfloat16 [4, 8192, 6144], P('pool', 'tp'), may hold values from -0.0625 to 0.0625
- expert_ids: int32 [3, 16, 2], P(None, 'grp'), parts along dimension 1, may hold values from 0 to 3, all different within a row; in each aligned block of 8 rows (0 to 7, 8 to 15, ..., all dimensions but the last counted through in order) at most 6 rows name the same one
Outputs:
- mixed_out: bfloat16 [3, 16, 6144], P(None, 'grp', ('pool', 'tp')), parts along dimension 1
The draws below stay inside these ranges and needn't reach their ends.
There are 2 independent parts, one for each index of `grp`. The reference program is written for one: setup_inputs(seed, part) draws one part's arguments, and reference() takes and returns one part's arrays. A program takes and returns all parts, laid end to end along the dimension named above; an argument that names none is the same for every part. Nothing has to cross between parts.
Inputs may be any that keep to these rules, and one draw needn't show every extreme that they name: `expert_ids`: in each micro-batch no expert is named by more than 6 tokens, and the two ids of a token differ. `cache_lengths`: the lengths of one micro-batch sum to 1024.
All inputs are finite; a program needn't handle non-finite values. No bound on the sum of `cache_lengths` on one device may be relied on, other than what follows from the above.
Results may differ from the reference program's by a relative error of at most 0.014.
Values may be sent and summed in bfloat16 or wider, within the bound.
A program may use at most 192 MiB of HBM per device.

```python
import math
import jax
import jax.numpy as jnp
import numpy as np
from jax import lax

D = 6144
HQ = 48
KVH = 8
HD = 128
EXPERTS = 4
FF = 8192
MB = 3
CTX = 256
GROUP = 1
SEQS = 8
CAP = 6


def draw_queries(key, part):
    key = jax.random.fold_in(key, 11)
    values = jax.random.truncated_normal(key, -5.0, 5.0, (MB, SEQS, KVH, HQ // KVH, HD))
    return values.reshape(MB, SEQS, HQ * HD).astype(jnp.bfloat16)


def draw_new_kv(key, part):
    key = jax.random.fold_in(key, 23)
    key_parts = jax.random.split(key, 2)
    new_keys = jax.random.truncated_normal(key_parts[0], -5.0, 5.0, (MB, SEQS, KVH, HD))
    new_values = jax.random.truncated_normal(key_parts[1], -5.0, 5.0, (MB, SEQS, KVH, HD))
    stacked = jnp.stack([new_keys.reshape(MB, SEQS, KVH * HD), new_values.reshape(MB, SEQS, KVH * HD)], axis=2)
    return stacked.astype(jnp.bfloat16)


def draw_kv_cache(key, part):
    key = jax.random.fold_in(key, 37)
    key_parts = jax.random.split(key, 2)
    cache_keys = jax.random.truncated_normal(key_parts[0], -5.0, 5.0, (MB, SEQS, CTX, KVH, HD))
    cache_values = jax.random.truncated_normal(key_parts[1], -5.0, 5.0, (MB, SEQS, CTX, KVH, HD))
    stacked = jnp.stack([cache_keys.reshape(MB, SEQS, CTX, KVH * HD), cache_values.reshape(MB, SEQS, CTX, KVH * HD)], axis=2)
    return stacked.astype(jnp.bfloat16)


def level_of(key, shape, cuts, low, high):
    factor_of, own = 1.0, jax.random.fold_in(key, 6)
    for axis_at, blocks in cuts:
        steps = jnp.exp(jax.random.uniform(jax.random.fold_in(own, axis_at), (blocks,), jnp.float32, low / len(cuts), high / len(cuts)))
        factor_of = factor_of * jnp.repeat(steps, shape[axis_at] // blocks).reshape([-1 if axis == axis_at else 1 for axis in range(len(shape))])
    return factor_of


def length_profile(number_of, total, bound, skew):
    portions = [(1 << 20) // math.isqrt(rank ** skew) + 1 for rank in range(2, number_of + 1)]
    surplus, holding = total - bound - (number_of - 1), [1] * (number_of - 1)
    while surplus > 0:
        movable = [i for i in range(number_of - 1) if holding[i] < bound]
        pool, left = sum([portions[i] for i in movable]), surplus
        for i in movable:
            more = min(bound - holding[i], max(1, left * portions[i] // pool), surplus)
            holding[i] = holding[i] + more
            surplus = surplus - more
    return np.array([bound] + holding)


def uneven_parts(key, number_of, total, bound, lean):
    if number_of == 2:
        one = jax.random.randint(key, (), max(1, total - bound), min(bound, total - 1) + 1)
        return jnp.stack([one, total - one])
    sizes = jnp.asarray(length_profile(number_of, total, bound, lean), jnp.int32)
    couples = (number_of - 1) // 2
    donor, receiver = sizes[1:1 + 2 * couples:2], sizes[2:2 + 2 * couples:2]
    margin = jnp.minimum(donor - 1, bound - receiver)
    shifted = jax.random.randint(jax.random.fold_in(key, 1), (couples,), 0, 1 << 20) % (margin + 1)
    sizes = sizes.at[1:1 + 2 * couples:2].set(donor - shifted).at[2:2 + 2 * couples:2].set(receiver + shifted)
    return sizes[jax.random.permutation(jax.random.fold_in(key, 2), number_of)]


def shared_out(rng, own, number, rows, number_of, top, reach, skew):
    sequence = jax.random.permutation(rng, number_of)
    crowded, ordinary = shares(number_of, rows * top, reach, skew, True), shares(number_of, rows * top, reach, skew, False)
    places = jnp.arange(number_of)

    def named(tallies, offset_by):
        used = int((tallies > 0).sum())
        fixed = max(1, used // 4)
        shifted = fixed + (places - fixed + offset_by * (used - fixed)) % max(1, number_of - fixed)
        return jnp.zeros((number_of,), jnp.int32).at[sequence[jnp.where(places < fixed, places, shifted)]].set(jnp.asarray(tallies, jnp.int32))

    tallies = jnp.where(number % 4 == 0, named(crowded, number // 4), named(ordinary, number - number // 4 - 1))
    mixed = jax.random.permutation(jax.random.fold_in(own, 3), number_of)
    source_of, taker = mixed[0:number_of // 2 * 2:2], mixed[1:number_of // 2 * 2:2]
    slack = jnp.minimum(tallies[source_of] - 1, reach - tallies[taker]) // 2
    slack = jnp.where((source_of == sequence[0]) | (taker == sequence[0]) | (tallies[taker] == 0), 0, jnp.maximum(slack, 0))
    shifted = jax.random.randint(jax.random.fold_in(own, 4), (number_of // 2,), 0, 1 << 20) % (slack + 1)
    tallies = tallies.at[source_of].add(-shifted).at[taker].add(shifted)
    members = jnp.searchsorted(jnp.cumsum(tallies), jnp.arange(rows * top), side="right").astype(jnp.int32)
    listing = members.reshape(top, rows).T
    listing = listing[jax.random.permutation(jax.random.fold_in(own, 1), rows)]
    offset_by = jax.random.randint(jax.random.fold_in(own, 2), (rows, 1), 0, top)
    return jnp.take_along_axis(listing, (jnp.arange(top)[None, :] + offset_by) % top, axis=1)


def shares(number_of, total, limit, lean, full):
    loads = [(1 << 20) // math.isqrt(grade ** lean) + 1 for grade in range(1, number_of + 1)]
    largest = limit if full else min(limit, max(-(-total // number_of), total * loads[0] // sum(loads)))
    least = 1 if total - largest >= number_of - 1 else 0
    holding, surplus = [largest] + [least] * (number_of - 1), total - largest - least * (number_of - 1)
    while surplus > 0:
        candidates = [i for i in range(1, number_of) if holding[i] < largest] or [i for i in range(1, number_of) if holding[i] < limit]
        pool, budget = sum([loads[i] for i in candidates]), surplus
        for i in candidates:
            addition = min(limit - holding[i], max(1, budget * loads[i] // pool), surplus)
            holding[i] = holding[i] + addition
            surplus = surplus - addition
    return np.array(holding)


def bell_draw(own_key, dims, spread, reach, shards=(), kind=jnp.bfloat16):
    array = spread * jax.random.normal(own_key, dims, jnp.float32)
    if shards:
        array = array * level_of(own_key, dims, shards, -0.22, 0.18)
    return jnp.clip(array, -reach, reach).astype(kind)


def setup_inputs(seed: int = 0, part: int = 0) -> dict:
    key_list = jax.random.split(jax.random.key(seed), 12)
    part_keys = jax.random.split(jax.random.fold_in(key_list[11], part), 12)
    queries = draw_queries(jax.random.fold_in(jax.random.fold_in(key_list[11], part), 71), part)
    new_kv = draw_new_kv(jax.random.fold_in(jax.random.fold_in(key_list[11], part), 71), part)
    kv_cache = draw_kv_cache(jax.random.fold_in(jax.random.fold_in(key_list[11], part), 71), part)
    cache_lengths = jax.vmap(lambda own: uneven_parts(own, SEQS, SEQS * CTX // 2, CTX, 2))(jax.random.split(part_keys[3], MB)).reshape((MB, SEQS)).astype(jnp.int32)
    residual_in = bell_draw(part_keys[4], (MB, SEQS, D), 1.0, 6.0, ((2, 16),))
    out_weight = bell_draw(key_list[5], (HQ * HD, D), (HQ * HD // 64) ** -0.5, 0.625, ((0, 4), (1, 4)))
    norm_gain = jnp.clip(1.0 + 0.18 * jax.random.normal(key_list[6], (D,), jnp.float32), 0.099609375, 1.8984375).astype(jnp.bfloat16)
    router_weight = bell_draw(key_list[7], (D, EXPERTS), D ** -0.5, 0.078125)
    expert_in = bell_draw(key_list[8], (EXPERTS * GROUP, 2, D, FF // GROUP), D ** -0.5, 0.078125, ((0, 4), (3, 4)))
    expert_out = bell_draw(key_list[9], (EXPERTS * GROUP, FF // GROUP, D), FF ** -0.5, 0.0625, ((0, 4), (1, 4)))
    expert_ids_keys = jax.random.split(jax.random.fold_in(part_keys[10], 1), MB * SEQS // SEQS)
    expert_ids_turns = jax.random.permutation(jax.random.fold_in(part_keys[10], 3), MB * SEQS // SEQS)
    expert_ids = jax.vmap(lambda own, number: shared_out(jax.random.fold_in(part_keys[10], 2), own, number, SEQS, EXPERTS, 2, CAP, 2))(expert_ids_keys, expert_ids_turns).reshape((MB, SEQS, 2))
    return {"queries": queries, "new_kv": new_kv, "kv_cache": kv_cache, "cache_lengths": cache_lengths, "residual_in": residual_in, "out_weight": out_weight, "norm_gain": norm_gain, "router_weight": router_weight, "expert_in": expert_in, "expert_out": expert_out, "expert_ids": expert_ids}


def attention(query_rows, new_pairs, cache_rows, lengths):
    seq_count = query_rows.shape[0]
    group_q = HQ // KVH
    query_heads = query_rows.astype(jnp.float32).reshape(seq_count, KVH, group_q, HD)
    key_rows = cache_rows[:, 0].astype(jnp.float32).reshape(seq_count, CTX, KVH, HD)
    value_rows = cache_rows[:, 1].astype(jnp.float32).reshape(seq_count, CTX, KVH, HD)
    new_keys = new_pairs[:, 0].astype(jnp.float32).reshape(seq_count, KVH, HD)
    new_values = new_pairs[:, 1].astype(jnp.float32).reshape(seq_count, KVH, HD)
    score_scale = 1.0 / math.sqrt(HD)
    old_scores = jnp.einsum('sgqd,scgd->sgqc', query_heads, key_rows) * score_scale
    new_scores = jnp.einsum('sgqd,sgd->sgq', query_heads, new_keys) * score_scale
    positions = jnp.arange(CTX, dtype=jnp.int32)
    valid_mask = positions[None, :] < lengths[:, None]
    old_scores = jnp.where(valid_mask[:, None, None, :], old_scores, -jnp.inf)
    row_max = jnp.maximum(lax.optimization_barrier(jnp.max(old_scores, axis=-1)), new_scores)
    old_exp = jnp.exp(old_scores - row_max[..., None])
    new_exp = jnp.exp(new_scores - row_max)
    row_total = lax.optimization_barrier(jnp.sum(old_exp, axis=-1)) + new_exp
    old_probs = (old_exp / row_total[..., None]).astype(jnp.bfloat16)
    new_probs = (new_exp / row_total).astype(jnp.bfloat16)
    attended = jnp.einsum('sgqc,scgd->sgqd', old_probs.astype(jnp.float32), value_rows)
    attended = attended + new_probs.astype(jnp.float32)[..., None] * new_values[:, :, None, :]
    return attended.reshape(seq_count, HQ * HD).astype(jnp.bfloat16)

def reference(queries, new_kv, kv_cache, cache_lengths, residual_in, out_weight, norm_gain, router_weight, expert_in, expert_out, expert_ids):
    outputs = []
    for micro_batch in range(MB):
        attended = attention(queries[micro_batch], new_kv[micro_batch], kv_cache[micro_batch], cache_lengths[micro_batch])
        projected = jnp.dot(attended, out_weight, preferred_element_type=jnp.float32)
        hidden = (residual_in[micro_batch].astype(jnp.float32) + projected).astype(jnp.bfloat16)
        hidden_f = hidden.astype(jnp.float32)
        mean_sq = lax.optimization_barrier(jnp.mean(hidden_f * hidden_f, axis=-1, keepdims=True))
        normed = (hidden_f * lax.rsqrt(mean_sq + 1e-05) * norm_gain.astype(jnp.float32)).astype(jnp.bfloat16)
        logits = jnp.dot(normed, router_weight, preferred_element_type=jnp.float32)
        chosen_ids = expert_ids[micro_batch]
        chosen_logits = jnp.take_along_axis(logits, chosen_ids, axis=1)
        weights = jax.nn.sigmoid(chosen_logits - chosen_logits[:, ::-1])
        mixture = jnp.zeros(hidden_f.shape, jnp.float32)
        for expert in range(EXPERTS):
            expert_sum = jnp.zeros(hidden_f.shape, jnp.float32)
            for member in range(GROUP):
                block = expert * GROUP + member
                gate_part = jnp.dot(normed, expert_in[block, 0], preferred_element_type=jnp.float32)
                up_part = jnp.dot(normed, expert_in[block, 1], preferred_element_type=jnp.float32)
                activated = (jax.nn.silu(gate_part) * up_part).astype(jnp.bfloat16)
                expert_sum = expert_sum + jnp.dot(activated, expert_out[block], preferred_element_type=jnp.float32)
            coeff = lax.optimization_barrier(jnp.sum(jnp.where(chosen_ids == expert, weights, 0.0), axis=1))
            mixture = mixture + coeff[:, None] * expert_sum
        outputs.append((hidden_f + mixture).astype(jnp.bfloat16))
    return jnp.stack(outputs)
```

```python
import functools
import math

import jax
import jax.numpy as jnp
from jax import lax
from jax.experimental import pallas as pl
from jax.experimental.pallas import tpu as pltpu
from jax.sharding import PartitionSpec as P

HQ = 48
KVH = 8
HD = 128


def attend(query_rows, new_pairs, cache_rows, lengths):
    seq_count = query_rows.shape[0]
    kv_local = new_pairs.shape[-1] // HD
    group_q = HQ // KVH
    cache_len = cache_rows.shape[2]
    query_heads = query_rows.reshape(seq_count, kv_local, group_q, HD)
    key_rows = cache_rows[:, 0].reshape(seq_count, cache_len, kv_local, HD)
    value_rows = cache_rows[:, 1].reshape(seq_count, cache_len, kv_local, HD)
    new_keys = new_pairs[:, 0].reshape(seq_count, kv_local, HD)
    new_values = new_pairs[:, 1].reshape(seq_count, kv_local, HD)
    score_scale = 1.0 / math.sqrt(HD)
    old_scores = (
        jnp.einsum("sgqd,scgd->sgqc", query_heads, key_rows, preferred_element_type=jnp.float32)
        * score_scale
    )
    new_scores = (
        jnp.einsum("sgqd,sgd->sgq", query_heads, new_keys, preferred_element_type=jnp.float32)
        * score_scale
    )
    positions = jnp.arange(cache_len, dtype=jnp.int32)
    valid_mask = positions[None, :] < lengths[:, None]
    old_scores = jnp.where(valid_mask[:, None, None, :], old_scores, -jnp.inf)
    row_max = jnp.maximum(jnp.max(old_scores, axis=-1), new_scores)
    old_exp = jnp.exp(old_scores - row_max[..., None])
    new_exp = jnp.exp(new_scores - row_max)
    row_total = jnp.sum(old_exp, axis=-1) + new_exp
    old_probs = (old_exp / row_total[..., None]).astype(jnp.bfloat16)
    new_probs = (new_exp / row_total).astype(jnp.bfloat16)
    attended = jnp.einsum(
        "sgqc,scgd->sgqd", old_probs, value_rows, preferred_element_type=jnp.float32
    )
    attended = (
        attended
        + new_probs.astype(jnp.float32)[..., None] * new_values.astype(jnp.float32)[:, :, None, :]
    )
    return attended.reshape(seq_count, kv_local * group_q * HD).astype(jnp.bfloat16)


def shards(
    queries,
    new_kv,
    kv_cache,
    cache_lengths,
    residual_in,
    out_weight,
    norm_gain,
    router_weight,
    expert_in,
    expert_out,
    expert_ids,
):
    experts = router_weight.shape[1]
    pool_count = lax.axis_size("pool")
    tp_count = lax.axis_size("tp")
    group_size = pool_count // experts
    own_expert = lax.axis_index("pool") // group_size
    batches = queries.shape[0]
    token_count = residual_in.shape[1]
    col_width = residual_in.shape[2]
    capacity = 3 * token_count // 4
    slots_all = jnp.arange(experts * capacity, dtype=jnp.int32)
    expert_range = jnp.arange(experts, dtype=jnp.int32)
    self_hot = (expert_range == own_expert).astype(jnp.float32)
    gain_f = norm_gain.astype(jnp.float32)
    hiddens = []
    pick_tables = []
    own_tables = []
    buffer_rows = []
    other_slots = []
    for micro_batch in range(batches):
        attended = attend(
            queries[micro_batch],
            new_kv[micro_batch],
            kv_cache[micro_batch],
            cache_lengths[micro_batch],
        )
        heads_out = jnp.dot(
            lax.all_gather(attended, "pool", axis=0, tiled=True),
            out_weight,
            preferred_element_type=jnp.float32,
        )
        summed = lax.psum_scatter(
            heads_out.reshape(token_count, tp_count, col_width),
            "tp",
            scatter_dimension=1,
            tiled=True,
        )
        hidden = (
            residual_in[micro_batch].astype(jnp.float32) + summed.reshape(token_count, col_width)
        ).astype(jnp.bfloat16)
        hiddens.append(hidden)
        chosen_ids = expert_ids[micro_batch]
        id_hot = (chosen_ids[:, :, None] == expert_range[None, None, :]).astype(jnp.int32)
        chosen = jnp.sum(id_hot, axis=1)
        before = jnp.cumsum(chosen, axis=0) - chosen
        slot_index = jnp.sum(id_hot * before[:, None, :], axis=2)
        buffer_row = chosen_ids * capacity + slot_index
        buffer_rows.append(buffer_row)
        pick_table = jnp.any(buffer_row[None, :, :] == slots_all[:, None, None], axis=2).astype(
            jnp.bfloat16
        )
        pick_tables.append(pick_table)
        own_table = lax.dynamic_slice_in_dim(pick_table, own_expert * capacity, capacity, 0)
        own_tables.append(own_table)
        other_ids = jnp.where(chosen_ids[:, 0] == own_expert, chosen_ids[:, 1], chosen_ids[:, 0])
        other_hot = (other_ids[:, None] == expert_range[None, :]).astype(jnp.bfloat16)
        other_slots.append(jnp.dot(own_table, other_hot, preferred_element_type=jnp.float32))
    packed = jnp.concatenate(
        [
            jnp.dot(pick_tables[b], hiddens[b], preferred_element_type=jnp.bfloat16).reshape(
                experts, capacity, col_width
            )
            for b in range(batches)
        ],
        axis=1,
    )
    outgoing = jnp.repeat(packed, group_size * tp_count, axis=0)
    expert_rows = lax.all_to_all(outgoing, ("pool", "tp"), split_axis=0, concat_axis=2, tiled=True)[
        0
    ]
    rows_f = expert_rows.astype(jnp.float32)
    mean_sq = jnp.mean(rows_f * rows_f, axis=-1, keepdims=True)
    normed = (rows_f * lax.rsqrt(mean_sq + 1e-05) * gain_f).astype(jnp.bfloat16)
    logits = jnp.dot(normed, router_weight, preferred_element_type=jnp.float32)
    other_slot = jnp.concatenate(other_slots, axis=0)
    logit_self = jnp.sum(logits * self_hot[None, :], axis=1)
    logit_other = jnp.sum(logits * other_slot, axis=1)
    weight = jax.nn.sigmoid(logit_self - logit_other)
    gate_up = jnp.einsum("cd,kdf->kcf", normed, expert_in[0], preferred_element_type=jnp.float32)
    activated = (jax.nn.silu(gate_up[0]) * gate_up[1]).astype(jnp.bfloat16)
    partial_value = (
        jnp.dot(activated, expert_out[0], preferred_element_type=jnp.float32) * weight[:, None]
    )
    returned = lax.all_to_all(
        partial_value, ("pool", "tp"), split_axis=1, concat_axis=0, tiled=True
    )
    merged = jnp.sum(
        returned.reshape(experts, group_size * tp_count, batches, capacity, col_width), axis=1
    )
    results = []
    for micro_batch in range(batches):
        merged_batch = merged[:, micro_batch].reshape(experts * capacity, col_width)
        combined = jnp.sum(
            jnp.take(merged_batch, buffer_rows[micro_batch].reshape(-1), axis=0).reshape(
                token_count, 2, col_width
            ),
            axis=1,
        )
        results.append((hiddens[micro_batch].astype(jnp.float32) + combined).astype(jnp.bfloat16))
    return jnp.stack(results)


MESH = pl.DeviceIdType.MESH
CHUNK = 256
NT = (((1,), (1,)), ((), ()))


def layer_kernel(
    sizes,
    lengths,
    q_hbm,
    nkv_hbm,
    kv_hbm,
    res_hbm,
    wo_hbm,
    gain_hbm,
    router_hbm,
    win_hbm,
    wout_hbm,
    ids_hbm,
    out_ref,
    q_v,
    nkv_v,
    kv_v,
    res_v,
    wo_v,
    gain_v,
    router_v,
    ids_v,
    slots,
    qrow,
    nkvf,
    qh,
    scores,
    probs,
    newp,
    att,
    att_all,
    att_rows,
    part_s,
    part_r,
    hid,
    hid_all,
    xn,
    act,
    mix_s,
    mix_r,
    mix_own,
    fin,
    fin_s,
    fin_r,
    small_sem,
    kv_sem,
    wo_sem,
    in_sem,
    out_sem,
    att_ss,
    att_rs,
    part_ss,
    part_rs,
    hid_ss,
    hid_rs,
    mix_ss,
    mix_rs,
    fin_ss,
    fin_rs,
):
    batches, seqs, kvl, group_q, hd, tokens, group_size = sizes
    pool_n, tp_n = 4, 4
    rows = batches * tokens
    col = res_v.shape[2]
    ffl = wout_hbm.shape[1]
    chunks = win_hbm.shape[3] // CHUNK
    half_w = mix_s.shape[3]
    per_half = half_w // CHUNK
    pool_w = tp_n * col

    p = lax.axis_index("pool")
    t = lax.axis_index("tp")
    flip = 1 - 2 * (p % 2)
    p_y = (p + 2) % 4
    p_c = p + flip
    p_yc = (p_y + flip) % 4
    mates = (p_y, p_yc, p_c)
    z_to = [(t + k) % tp_n for k in range(1, tp_n)]
    z_from = [(t + tp_n - k) % tp_n for k in range(1, tp_n)]

    barrier = pltpu.get_barrier_semaphore()
    for mate in mates:
        pl.semaphore_signal(barrier, inc=1, device_id={"pool": mate}, device_id_type=MESH)
    for peer in z_to:
        pl.semaphore_signal(barrier, inc=1, device_id={"tp": peer}, device_id_type=MESH)

    smalls = [
        pltpu.make_async_copy(src, dst, small_sem.at[i])
        for i, (src, dst) in enumerate(
            [
                (q_hbm, q_v),
                (nkv_hbm, nkv_v),
                (res_hbm, res_v),
                (gain_hbm, gain_v),
                (router_hbm, router_v),
                (ids_hbm, ids_v),
            ]
        )
    ]
    for copy in smalls[:2]:
        copy.start()
    kv_copy = pltpu.make_async_copy(kv_hbm, kv_v, kv_sem)
    kv_copy.start()
    for copy in smalls[2:]:
        copy.start()
    wo_copies = [
        pltpu.make_async_copy(wo_hbm.at[:, pl.ds(k * col, col)], wo_v.at[k], wo_sem.at[k])
        for k in range(tp_n)
    ]
    for copy in wo_copies:
        copy.start()

    def in_copy(j):
        return pltpu.make_async_copy(
            win_hbm.at[0, :, :, pl.ds(pl.multiple_of(j * CHUNK, CHUNK), CHUNK)],
            slots.at[j],
            in_sem.at[j],
        )

    def out_copy(slot, half, c, pool_block):
        start = pool_block * pool_w + half * half_w + c * CHUNK
        return pltpu.make_async_copy(
            wout_hbm.at[0, :, pl.ds(pl.multiple_of(start, CHUNK), CHUNK)],
            slots.at[slot, half, pl.ds(c * ffl, ffl), :],
            out_sem.at[slot, half, c],
        )

    for copy in smalls[:2]:
        copy.wait()
    att[...] = jnp.zeros_like(att)
    qh[...] = jnp.zeros_like(qh)
    for b in range(batches):
        qrow[pl.ds(b * seqs, seqs), :] = q_v[b].astype(jnp.float32)
    for b in range(batches):
        for s in range(seqs):
            nkvf[b * seqs + s] = nkv_v[b, s].astype(jnp.float32)
    for r in range(batches * seqs):
        for g in range(kvl):
            for h in range(group_q):
                qh[pl.ds((r * kvl + g) * 8 + h, 1), :] = qrow[
                    pl.ds(r, 1), pl.ds((g * group_q + h) * hd, hd)
                ]
    kv_copy.wait()

    @pl.loop(0, chunks)
    def _(j):
        in_copy(j).start()

    ctx = kv_v.shape[3]
    scale = 1.0 / math.sqrt(hd)
    place = lax.broadcasted_iota(jnp.int32, (8, ctx), 1)
    news = []
    for r in range(batches * seqs):
        b, s = r // seqs, r % seqs
        for g in range(kvl):
            q8 = qh[pl.ds((r * kvl + g) * 8, 8), :]
            keys = kv_v[b, s, 0, :, g * hd : (g + 1) * hd]
            sc = (
                lax.dot_general(
                    q8.astype(jnp.bfloat16), keys, NT, preferred_element_type=jnp.float32
                )
                * scale
            )
            scores[pl.ds((r * kvl + g) * 8, 8), :] = jnp.where(
                place < lengths[b, s], sc, -jnp.inf
            )
            nk = nkvf[r, 0:1, g * hd : (g + 1) * hd]
            news.append(jnp.sum(q8 * nk, axis=1, keepdims=True) * scale)
    new = jnp.concatenate(news, axis=0)
    old = scores[...]
    top = jnp.maximum(jnp.max(old, axis=1, keepdims=True), new)
    old_exp = jnp.exp(old - top)
    new_exp = jnp.exp(new - top)
    total = jnp.sum(old_exp, axis=1, keepdims=True) + new_exp
    probs[...] = old_exp / total
    newp[...] = jnp.broadcast_to(
        (new_exp / total).astype(jnp.bfloat16).astype(jnp.float32), newp.shape
    )
    for r in range(batches * seqs):
        b, s = r // seqs, r % seqs
        for g in range(kvl):
            at = pl.ds((r * kvl + g) * 8, 8)
            values = kv_v[b, s, 1, :, g * hd : (g + 1) * hd]
            o8 = jnp.dot(
                probs[at, :].astype(jnp.bfloat16), values, preferred_element_type=jnp.float32
            )
            o8 = o8 + newp[at, :] * nkvf[r, 1:2, g * hd : (g + 1) * hd]
            for h in range(group_q):
                att[r : r + 1, (g * group_q + h) * hd : (g * group_q + h + 1) * hd] = o8[h : h + 1]
    att_all[p] = att[...].astype(jnp.bfloat16)

    pl.semaphore_wait(barrier, len(mates) + len(z_to))

    def send(src, dst, ss, rs, where):
        return pltpu.make_async_remote_copy(
            src_ref=src, dst_ref=dst, send_sem=ss, recv_sem=rs, device_id=where,
            device_id_type=MESH,
        )

    sent = []
    att_copies = []
    for i, mate in enumerate(mates):
        copy = send(att_all.at[p], att_all.at[p], att_ss.at[i], att_rs.at[i], {"pool": mate})
        copy.start()
        att_copies.append(copy)
    for copy in wo_copies:
        copy.wait()
    for i, mate in enumerate(mates):
        send(
            att_all.at[mate], att_all.at[mate], att_ss.at[i], att_rs.at[i], {"pool": mate}
        ).wait_recv()
    sent += att_copies
    for m in range(pool_n):
        x = att_all[m].astype(jnp.float32)
        for b in range(batches):
            att_rows[pl.ds(b * tokens + m * seqs, seqs), :] = x[b * seqs : (b + 1) * seqs]
    lhs = att_rows[...].astype(jnp.bfloat16)

    for i, peer in enumerate(z_to):
        part_s[i] = jnp.dot(lhs, wo_v[peer], preferred_element_type=jnp.float32).astype(
            jnp.bfloat16
        )
        copy = send(part_s.at[i], part_r.at[i], part_ss.at[i], part_rs.at[i], {"tp": peer})
        copy.start()
        sent.append(copy)
    summed = jnp.dot(lhs, wo_v[t], preferred_element_type=jnp.float32)
    for copy in smalls[2:]:
        copy.wait()
    res = jnp.concatenate([res_v[b].astype(jnp.float32) for b in range(batches)], axis=0)
    summed = summed + res
    for i, peer in enumerate(z_to):
        send(
            part_s.at[i], part_r.at[i], part_ss.at[i], part_rs.at[i], {"tp": peer}
        ).wait_recv()
        summed = summed + part_r[i].astype(jnp.float32)
    hidden = summed.astype(jnp.bfloat16)
    hid[...] = hidden.astype(jnp.float32)
    hid_all[p, t] = hidden

    def hid_send(pp, tt, n, where):
        return send(
            hid_all.at[pp, tt], hid_all.at[pp, tt], hid_ss.at[n], hid_rs.at[pp, tt], where
        )

    for i, peer in enumerate(z_to):
        copy = hid_send(p, t, i, {"tp": peer})
        copy.start()
        sent.append(copy)
    order = [t] + z_from
    n = tp_n - 1
    for i, tt in enumerate(order):
        if i > 0:
            hid_send(p, tt, i - 1, {"tp": tt}).wait_recv()
        for mate in (p_y, p_c):
            copy = hid_send(p, tt, n, {"pool": mate})
            copy.start()
            sent.append(copy)
            n += 1
    for tt in order:
        hid_send(p_y, tt, 0, {"pool": p_y}).wait_recv()
        copy = hid_send(p_y, tt, n, {"pool": p_c})
        copy.start()
        sent.append(copy)
        n += 1
    for tt in order:
        hid_send(p_c, tt, 0, {"pool": p_c}).wait_recv()
    for tt in order:
        hid_send(p_yc, tt, 0, {"pool": p_c}).wait_recv()

    squares = jnp.zeros((rows, col), jnp.float32)
    for m in range(pool_n):
        for tt in range(tp_n):
            h = hid_all[m, tt].astype(jnp.float32)
            squares = squares + h * h
    inv = lax.rsqrt(jnp.sum(squares, axis=1, keepdims=True) / (pool_n * pool_w) + 1e-05)
    for m in range(pool_n):
        for tt in range(tp_n):
            h = hid_all[m, tt].astype(jnp.float32)
            at = pl.ds((m * tp_n + tt) * col, col)
            xn[:, at] = (h * inv * gain_v[:, at].astype(jnp.float32)).astype(jnp.bfloat16)
    logits = lax.dot_general(xn[...], router_v[...], NT, preferred_element_type=jnp.float32)
    experts = router_v.shape[0]
    own = p // group_size
    lane = lax.broadcasted_iota(jnp.int32, (tokens, experts), 1)
    coeffs = []
    for b in range(batches):
        lb = logits[b * tokens : (b + 1) * tokens]
        id0 = ids_v[b, :, 0:1]
        id1 = ids_v[b, :, 1:2]
        l0 = jnp.sum(jnp.where(lane == id0, lb, 0.0), axis=1, keepdims=True)
        l1 = jnp.sum(jnp.where(lane == id1, lb, 0.0), axis=1, keepdims=True)
        coeffs.append(
            jnp.where(id0 == own, jax.nn.sigmoid(l0 - l1), 0.0)
            + jnp.where(id1 == own, jax.nn.sigmoid(l1 - l0), 0.0)
        )
    coeff = jnp.concatenate(coeffs, axis=0)

    def gate_up(j):
        in_copy(j).wait()
        gate = jnp.dot(xn[...], slots[j, 0], preferred_element_type=jnp.float32)
        up = jnp.dot(xn[...], slots[j, 1], preferred_element_type=jnp.float32)
        act[:, pl.ds(pl.multiple_of(j * CHUNK, CHUNK), CHUNK)] = (
            jax.nn.silu(gate) * up
        ).astype(jnp.bfloat16)

    targets = mates + (p,)
    for j in range(len(targets)):
        gate_up(j)
        for half in range(2):
            for c in range(per_half):
                out_copy(j, half, c, targets[j]).start()

    @pl.loop(len(targets), chunks)
    def _(j):
        gate_up(j)

    def down(slot, half, c):
        out_copy(slot, half, c, targets[slot]).wait()
        return (
            jnp.dot(
                act[...],
                slots[slot, half, c * ffl : (c + 1) * ffl, :],
                preferred_element_type=jnp.float32,
            )
            * coeff
        )

    for i, mate in enumerate(mates):
        for half in range(2):
            for c in range(per_half):
                mix_s[i, half, :, c * CHUNK : (c + 1) * CHUNK] = down(i, half, c).astype(
                    jnp.bfloat16
                )
            copy = send(
                mix_s.at[i, half],
                mix_r.at[i, half],
                mix_ss.at[i, half],
                mix_rs.at[i, half],
                {"pool": mate},
            )
            copy.start()
            sent.append(copy)
    for half in range(2):
        for c in range(per_half):
            mix_own[half, :, c * CHUNK : (c + 1) * CHUNK] = down(len(mates), half, c)
    for i, mate in enumerate(mates):
        for half in range(2):
            send(
                mix_s.at[i, half],
                mix_r.at[i, half],
                mix_ss.at[i, half],
                mix_rs.at[i, half],
                {"pool": mate},
            ).wait_recv()
    for half in range(2):
        whole = mix_own[half]
        for i in range(len(mates)):
            whole = whole + mix_r[i, half].astype(jnp.float32)
        for k in range(2):
            piece = whole[:, k * col : (k + 1) * col]
            fin[half * 2 + k] = piece
            fin_s[half * 2 + k] = piece.astype(jnp.bfloat16)
    for i, peer in enumerate(z_to):
        copy = send(fin_s.at[peer], fin_r.at[i], fin_ss.at[i], fin_rs.at[i], {"tp": peer})
        copy.start()
        sent.append(copy)
    result = hid[...] + fin[t]
    for i, peer in enumerate(z_to):
        send(fin_s.at[peer], fin_r.at[i], fin_ss.at[i], fin_rs.at[i], {"tp": peer}).wait_recv()
        result = result + fin_r[i].astype(jnp.float32)
    for b in range(batches):
        out_ref[b] = result[b * tokens : (b + 1) * tokens].astype(jnp.bfloat16)
    for copy in sent:
        copy.wait_send()


def fused(
    queries,
    new_kv,
    kv_cache,
    cache_lengths,
    residual_in,
    out_weight,
    norm_gain,
    router_weight,
    expert_in,
    expert_out,
    expert_ids,
):
    batches, seqs, q_width = queries.shape
    tokens, col = residual_in.shape[1:]
    rows = batches * tokens
    kvl = new_kv.shape[3] // HD
    group_q = HQ // KVH
    model = norm_gain.shape[0]
    experts = router_weight.shape[1]
    ffl = expert_out.shape[1]
    ctx = kv_cache.shape[3]
    tp_n = 4
    heads = batches * seqs * kvl * 8
    half_w = tp_n * col // 2
    per_half = half_w // CHUNK
    chunks = ffl // CHUNK
    bf, f32 = jnp.bfloat16, jnp.float32
    dma = pltpu.SemaphoreType.DMA
    sizes = (batches, seqs, kvl, group_q, HD, tokens, 4 // experts)
    return pl.pallas_call(
        functools.partial(layer_kernel, sizes),
        out_shape=jax.ShapeDtypeStruct(residual_in.shape, bf),
        in_specs=[pl.BlockSpec(memory_space=pltpu.SMEM)]
        + [pl.BlockSpec(memory_space=pl.ANY)] * 10,
        out_specs=pl.BlockSpec(memory_space=pltpu.VMEM),
        scratch_shapes=[
            pltpu.VMEM(queries.shape, bf),
            pltpu.VMEM(new_kv.shape, bf),
            pltpu.VMEM(kv_cache.shape, bf),
            pltpu.VMEM(residual_in.shape, bf),
            pltpu.VMEM((tp_n, q_width, col), bf),
            pltpu.VMEM((1, model), bf),
            pltpu.VMEM((experts, model), bf),
            pltpu.VMEM(expert_ids.shape, jnp.int32),
            pltpu.VMEM((chunks, 2, model, CHUNK), bf),
            pltpu.VMEM((8, q_width), f32),
            pltpu.VMEM((batches * seqs, 2, kvl * HD), f32),
            pltpu.VMEM((heads, HD), f32),
            pltpu.VMEM((heads, ctx), f32),
            pltpu.VMEM((heads, ctx), f32),
            pltpu.VMEM((heads, HD), f32),
            pltpu.VMEM((8, q_width), f32),
            pltpu.VMEM((4, 8, q_width), bf),
            pltpu.VMEM((rows, q_width), f32),
            pltpu.VMEM((tp_n - 1, rows, col), bf),
            pltpu.VMEM((tp_n - 1, rows, col), bf),
            pltpu.VMEM((rows, col), f32),
            pltpu.VMEM((4, tp_n, rows, col), bf),
            pltpu.VMEM((rows, model), bf),
            pltpu.VMEM((rows, ffl), bf),
            pltpu.VMEM((3, 2, rows, half_w), bf),
            pltpu.VMEM((3, 2, rows, half_w), bf),
            pltpu.VMEM((2, rows, half_w), f32),
            pltpu.VMEM((tp_n, rows, col), f32),
            pltpu.VMEM((tp_n, rows, col), bf),
            pltpu.VMEM((tp_n - 1, rows, col), bf),
            dma((6,)),
            dma,
            dma((tp_n,)),
            dma((chunks,)),
            dma((4, 2, per_half)),
            dma((3,)),
            dma((3,)),
            dma((tp_n - 1,)),
            dma((tp_n - 1,)),
            dma((15,)),
            dma((4, tp_n)),
            dma((3, 2)),
            dma((3, 2)),
            dma((tp_n - 1,)),
            dma((tp_n - 1,)),
        ],
        compiler_params=pltpu.CompilerParams(
            collective_id=0, has_side_effects=True, vmem_limit_bytes=60 * 1024 * 1024
        ),
        cost_estimate=pl.CostEstimate(
            flops=6 * rows * model * ffl,
            bytes_accessed=6 * model * ffl + 2 * out_weight.size,
            transcendentals=0,
        ),
        name="layer",
    )(
        cache_lengths,
        queries,
        new_kv,
        kv_cache,
        residual_in,
        out_weight,
        norm_gain.reshape(1, model),
        router_weight.T,
        expert_in,
        expert_out,
        expert_ids,
    )


def body(*arrays):
    queries, new_kv, _, _, residual_in, _, norm_gain, router_weight, _, expert_out, _ = arrays
    ffl, model = expert_out.shape[1:]
    col = residual_in.shape[2]
    fits = (
        lax.axis_size("pool") == 4
        and lax.axis_size("tp") == 4
        and 4 % router_weight.shape[1] == 0
        and col % 128 == 0
        and (2 * col) % CHUNK == 0
        and ffl % CHUNK == 0
        and ffl // CHUNK >= 4
        and 4 * col // CHUNK * ffl == 2 * model
        and queries.shape[0] * queries.shape[1] <= 8
        and residual_in.shape[1] % 8 == 0
    )
    return fused(*arrays) if fits else shards(*arrays)


def solution(mesh):
    return jax.shard_map(
        body,
        mesh=mesh,
        in_specs=(
            P(None, ("grp", "pool"), "tp"),
            P(None, ("grp", "pool"), None, "tp"),
            P(None, ("grp", "pool"), None, None, "tp"),
            P(None, ("grp", "pool")),
            P(None, "grp", ("pool", "tp")),
            P("tp", "pool"),
            P(),
            P(),
            P("pool", None, None, "tp"),
            P("pool", "tp", None),
            P(None, "grp", None),
        ),
        out_specs=P(None, "grp", ("pool", "tp")),
        check_vma=False,
    )
```

```python
import functools
import math

import jax
import jax.numpy as jnp
from jax import lax
from jax.experimental import pallas as pl
from jax.experimental.pallas import tpu as pltpu
from jax.sharding import PartitionSpec as P

HQ = 48
KVH = 8
HD = 128


def attend(query_rows, new_pairs, cache_rows, lengths):
    seq_count = query_rows.shape[0]
    kv_local = new_pairs.shape[-1] // HD
    group_q = HQ // KVH
    cache_len = cache_rows.shape[2]
    query_heads = query_rows.reshape(seq_count, kv_local, group_q, HD)
    key_rows = cache_rows[:, 0].reshape(seq_count, cache_len, kv_local, HD)
    value_rows = cache_rows[:, 1].reshape(seq_count, cache_len, kv_local, HD)
    new_keys = new_pairs[:, 0].reshape(seq_count, kv_local, HD)
    new_values = new_pairs[:, 1].reshape(seq_count, kv_local, HD)
    score_scale = 1.0 / math.sqrt(HD)
    old_scores = (
        jnp.einsum("sgqd,scgd->sgqc", query_heads, key_rows, preferred_element_type=jnp.float32)
        * score_scale
    )
    new_scores = (
        jnp.einsum("sgqd,sgd->sgq", query_heads, new_keys, preferred_element_type=jnp.float32)
        * score_scale
    )
    positions = jnp.arange(cache_len, dtype=jnp.int32)
    valid_mask = positions[None, :] < lengths[:, None]
    old_scores = jnp.where(valid_mask[:, None, None, :], old_scores, -jnp.inf)
    row_max = jnp.maximum(jnp.max(old_scores, axis=-1), new_scores)
    old_exp = jnp.exp(old_scores - row_max[..., None])
    new_exp = jnp.exp(new_scores - row_max)
    row_total = jnp.sum(old_exp, axis=-1) + new_exp
    old_probs = (old_exp / row_total[..., None]).astype(jnp.bfloat16)
    new_probs = (new_exp / row_total).astype(jnp.bfloat16)
    attended = jnp.einsum(
        "sgqc,scgd->sgqd", old_probs, value_rows, preferred_element_type=jnp.float32
    )
    attended = (
        attended
        + new_probs.astype(jnp.float32)[..., None] * new_values.astype(jnp.float32)[:, :, None, :]
    )
    return attended.reshape(seq_count, kv_local * group_q * HD).astype(jnp.bfloat16)


def shards(
    queries,
    new_kv,
    kv_cache,
    cache_lengths,
    residual_in,
    out_weight,
    norm_gain,
    router_weight,
    expert_in,
    expert_out,
    expert_ids,
):
    experts = router_weight.shape[1]
    pool_count = lax.axis_size("pool")
    tp_count = lax.axis_size("tp")
    group_size = pool_count // experts
    own_expert = lax.axis_index("pool") // group_size
    batches = queries.shape[0]
    token_count = residual_in.shape[1]
    col_width = residual_in.shape[2]
    capacity = 3 * token_count // 4
    slots_all = jnp.arange(experts * capacity, dtype=jnp.int32)
    expert_range = jnp.arange(experts, dtype=jnp.int32)
    self_hot = (expert_range == own_expert).astype(jnp.float32)
    gain_f = norm_gain.astype(jnp.float32)
    hiddens = []
    pick_tables = []
    own_tables = []
    buffer_rows = []
    other_slots = []
    for micro_batch in range(batches):
        attended = attend(
            queries[micro_batch],
            new_kv[micro_batch],
            kv_cache[micro_batch],
            cache_lengths[micro_batch],
        )
        heads_out = jnp.dot(
            lax.all_gather(attended, "pool", axis=0, tiled=True),
            out_weight,
            preferred_element_type=jnp.float32,
        )
        summed = lax.psum_scatter(
            heads_out.reshape(token_count, tp_count, col_width),
            "tp",
            scatter_dimension=1,
            tiled=True,
        )
        hidden = (
            residual_in[micro_batch].astype(jnp.float32) + summed.reshape(token_count, col_width)
        ).astype(jnp.bfloat16)
        hiddens.append(hidden)
        chosen_ids = expert_ids[micro_batch]
        id_hot = (chosen_ids[:, :, None] == expert_range[None, None, :]).astype(jnp.int32)
        chosen = jnp.sum(id_hot, axis=1)
        before = jnp.cumsum(chosen, axis=0) - chosen
        slot_index = jnp.sum(id_hot * before[:, None, :], axis=2)
        buffer_row = chosen_ids * capacity + slot_index
        buffer_rows.append(buffer_row)
        pick_table = jnp.any(buffer_row[None, :, :] == slots_all[:, None, None], axis=2).astype(
            jnp.bfloat16
        )
        pick_tables.append(pick_table)
        own_table = lax.dynamic_slice_in_dim(pick_table, own_expert * capacity, capacity, 0)
        own_tables.append(own_table)
        other_ids = jnp.where(chosen_ids[:, 0] == own_expert, chosen_ids[:, 1], chosen_ids[:, 0])
        other_hot = (other_ids[:, None] == expert_range[None, :]).astype(jnp.bfloat16)
        other_slots.append(jnp.dot(own_table, other_hot, preferred_element_type=jnp.float32))
    packed = jnp.concatenate(
        [
            jnp.dot(pick_tables[b], hiddens[b], preferred_element_type=jnp.bfloat16).reshape(
                experts, capacity, col_width
            )
            for b in range(batches)
        ],
        axis=1,
    )
    outgoing = jnp.repeat(packed, group_size * tp_count, axis=0)
    expert_rows = lax.all_to_all(outgoing, ("pool", "tp"), split_axis=0, concat_axis=2, tiled=True)[
        0
    ]
    rows_f = expert_rows.astype(jnp.float32)
    mean_sq = jnp.mean(rows_f * rows_f, axis=-1, keepdims=True)
    normed = (rows_f * lax.rsqrt(mean_sq + 1e-05) * gain_f).astype(jnp.bfloat16)
    logits = jnp.dot(normed, router_weight, preferred_element_type=jnp.float32)
    other_slot = jnp.concatenate(other_slots, axis=0)
    logit_self = jnp.sum(logits * self_hot[None, :], axis=1)
    logit_other = jnp.sum(logits * other_slot, axis=1)
    weight = jax.nn.sigmoid(logit_self - logit_other)
    gate_up = jnp.einsum("cd,kdf->kcf", normed, expert_in[0], preferred_element_type=jnp.float32)
    activated = (jax.nn.silu(gate_up[0]) * gate_up[1]).astype(jnp.bfloat16)
    partial_value = (
        jnp.dot(activated, expert_out[0], preferred_element_type=jnp.float32) * weight[:, None]
    )
    returned = lax.all_to_all(
        partial_value, ("pool", "tp"), split_axis=1, concat_axis=0, tiled=True
    )
    merged = jnp.sum(
        returned.reshape(experts, group_size * tp_count, batches, capacity, col_width), axis=1
    )
    results = []
    for micro_batch in range(batches):
        merged_batch = merged[:, micro_batch].reshape(experts * capacity, col_width)
        combined = jnp.sum(
            jnp.take(merged_batch, buffer_rows[micro_batch].reshape(-1), axis=0).reshape(
                token_count, 2, col_width
            ),
            axis=1,
        )
        results.append((hiddens[micro_batch].astype(jnp.float32) + combined).astype(jnp.bfloat16))
    return jnp.stack(results)


MESH = pl.DeviceIdType.MESH
CHUNK = 256
NT = (((1,), (1,)), ((), ()))


def layer_kernel(
    sizes,
    len_hbm,
    q_hbm,
    nkv_hbm,
    kv_hbm,
    res_hbm,
    wo_hbm,
    gain_hbm,
    router_hbm,
    win_hbm,
    wout_hbm,
    ids_hbm,
    out_ref,
    lengths,
    q_v,
    nkv_v,
    kv_v,
    res_v,
    gain_v,
    router_v,
    ids_v,
    slots,
    att,
    nkvf,
    qh,
    scores,
    newp,
    att_all,
    att_rows,
    part_s,
    part_r,
    hid,
    hid_all,
    gain_f,
    xn,
    acc,
    act,
    mix_s,
    mix_r,
    small_sem,
    kv_sem,
    wo_sem,
    in_sem,
    out_sem,
    att_ss,
    att_rs,
    part_ss,
    part_rs,
    hid_ss,
    hid_rs,
    mix_ss,
    mix_rs,
):
    batches, seqs, kvl, group_q, hd, tokens, group_size = sizes
    pool_n, tp_n = 4, 4
    rows = batches * tokens
    col = res_v.shape[2]
    ffl = wout_hbm.shape[1]
    chunks = win_hbm.shape[3] // CHUNK
    half_w = 2 * col
    per_half = half_w // CHUNK
    pool_w = tp_n * col

    p = lax.axis_index("pool")
    t = lax.axis_index("tp")
    flip = 1 - 2 * (p % 2)
    p_y = (p + 2) % 4
    p_c = p + flip
    p_yc = (p_y + flip) % 4
    mates = (p_y, p_yc, p_c)
    z_to = [(t + k) % tp_n for k in range(1, tp_n)]
    z_from = [(t + tp_n - k) % tp_n for k in range(1, tp_n)]

    barrier = pltpu.get_barrier_semaphore()
    targets = mates + (p,)
    others = [(m, z) for m in targets for z in z_to + [t]][:-1]
    for mate, peer in others:
        pl.semaphore_signal(
            barrier, inc=1, device_id={"pool": mate, "tp": peer}, device_id_type=MESH
        )

    smalls = [
        pltpu.make_async_copy(src, dst, small_sem.at[i])
        for i, (src, dst) in enumerate(
            [
                (q_hbm, q_v),
                (nkv_hbm, nkv_v),
                (len_hbm, lengths),
                (res_hbm, res_v),
                (gain_hbm, gain_v),
                (router_hbm, router_v),
                (ids_hbm, ids_v),
            ]
        )
    ]
    for copy in smalls[:3]:
        copy.start()
    kv_copy = pltpu.make_async_copy(kv_hbm, kv_v, kv_sem)
    kv_copy.start()
    for copy in smalls[3:]:
        copy.start()
    q_width = wo_hbm.shape[0]
    stack = slots.shape[2] // q_width

    def wo_at(c):
        return slots.at[chunks, c // stack, pl.ds(c % stack * q_width, q_width), :]

    wo_copies = [
        pltpu.make_async_copy(wo_hbm.at[:, pl.ds(c * CHUNK, CHUNK)], wo_at(c), wo_sem.at[c])
        for c in range(pool_w // CHUNK)
    ]
    for copy in wo_copies:
        copy.start()

    def in_copy(j):
        return pltpu.make_async_copy(
            win_hbm.at[0, :, :, pl.ds(pl.multiple_of(j * CHUNK, CHUNK), CHUNK)],
            slots.at[j],
            in_sem.at[j],
        )

    far, near = 1 - t // 2, t // 2
    groups = [(i, h) for h in (far, near) for i in range(pool_n)]
    places = [chunks, 0, 1, 2]

    def out_copy(n, c):
        start = targets[groups[n][0]] * pool_w + groups[n][1] * half_w + c * CHUNK
        return pltpu.make_async_copy(
            wout_hbm.at[0, :, pl.ds(pl.multiple_of(start, CHUNK), CHUNK)],
            slots.at[places[n // 2], n % 2, pl.ds(c * ffl, ffl), :],
            out_sem.at[n, c],
        )

    def start_pair(pair):
        for n in (2 * pair, 2 * pair + 1):
            for c in range(per_half):
                out_copy(n, c).start()

    for copy in smalls[:3]:
        copy.wait()
    qh[...] = jnp.zeros_like(qh)
    for b in range(batches):
        att[pl.ds(b * seqs, seqs), :] = q_v[b].astype(jnp.float32)
    for b in range(batches):
        for s in range(seqs):
            nkvf[b * seqs + s] = nkv_v[b, s].astype(jnp.float32)
    for r in range(batches * seqs):
        for g in range(kvl):
            for h in range(group_q):
                qh[pl.ds((r * kvl + g) * 8 + h, 1), :] = att[
                    pl.ds(r, 1), pl.ds((g * group_q + h) * hd, hd)
                ]
    att[...] = jnp.zeros_like(att)
    kv_copy.wait()

    @pl.loop(0, chunks)
    def _(j):
        in_copy(j).start()
    ctx = kv_v.shape[3]
    scale = 1.0 / math.sqrt(hd)
    place = lax.broadcasted_iota(jnp.int32, (8, ctx), 1)
    news = []
    for r in range(batches * seqs):
        b, s = r // seqs, r % seqs
        for g in range(kvl):
            q8 = qh[pl.ds((r * kvl + g) * 8, 8), :]
            keys = kv_v[b, s, 0, :, g * hd : (g + 1) * hd]
            sc = (
                lax.dot_general(
                    q8.astype(jnp.bfloat16), keys, NT, preferred_element_type=jnp.float32
                )
                * scale
            )
            scores[pl.ds((r * kvl + g) * 8, 8), :] = jnp.where(
                place < lengths[s, b], sc, -jnp.inf
            )
            nk = nkvf[r, 0:1, g * hd : (g + 1) * hd]
            news.append(jnp.sum(q8 * nk, axis=1, keepdims=True) * scale)
    new = jnp.concatenate(news, axis=0)
    old = scores[...]
    top = jnp.maximum(jnp.max(old, axis=1, keepdims=True), new)
    old_exp = jnp.exp(old - top)
    new_exp = jnp.exp(new - top)
    total = jnp.sum(old_exp, axis=1, keepdims=True) + new_exp
    scores[...] = old_exp / total
    newp[...] = jnp.broadcast_to(
        (new_exp / total).astype(jnp.bfloat16).astype(jnp.float32), newp.shape
    )
    for r in range(batches * seqs):
        b, s = r // seqs, r % seqs
        for g in range(kvl):
            at = pl.ds((r * kvl + g) * 8, 8)
            values = kv_v[b, s, 1, :, g * hd : (g + 1) * hd]
            o8 = jnp.dot(
                scores[at, :].astype(jnp.bfloat16), values, preferred_element_type=jnp.float32
            )
            o8 = o8 + newp[at, :] * nkvf[r, 1:2, g * hd : (g + 1) * hd]
            for h in range(group_q):
                att[r : r + 1, (g * group_q + h) * hd : (g * group_q + h + 1) * hd] = o8[h : h + 1]
    att_all[p] = att[...].astype(jnp.bfloat16)

    pl.semaphore_wait(barrier, len(others))

    def send(src, dst, ss, rs, where):
        return pltpu.make_async_remote_copy(
            src_ref=src, dst_ref=dst, send_sem=ss, recv_sem=rs, device_id=where,
            device_id_type=MESH,
        )

    sent = []
    att_copies = []
    for i, mate in enumerate(mates):
        copy = send(att_all.at[p], att_all.at[p], att_ss.at[i], att_rs.at[i], {"pool": mate})
        copy.start()
        att_copies.append(copy)
    for copy in wo_copies:
        copy.wait()
    for i, mate in enumerate(mates):
        send(
            att_all.at[mate], att_all.at[mate], att_ss.at[i], att_rs.at[i], {"pool": mate}
        ).wait_recv()
    sent += att_copies
    for m in range(pool_n):
        x = att_all[m].astype(jnp.float32)
        for b in range(batches):
            att_rows[pl.ds(b * tokens + m * seqs, seqs), :] = x[b * seqs : (b + 1) * seqs]
    lhs = att_rows[...].astype(jnp.bfloat16)

    for c in range(pool_w // CHUNK):
        att_rows[:, c * CHUNK : (c + 1) * CHUNK] = jnp.dot(
            lhs, wo_at(c)[...], preferred_element_type=jnp.float32
        )

    def piece_of(who):
        return att_rows[:, pl.ds(pl.multiple_of(who * col, col), col)]

    for i, peer in enumerate(z_to):
        part_s[i] = piece_of(peer).astype(jnp.bfloat16)
        copy = send(part_s.at[i], part_r.at[i], part_ss.at[i], part_rs.at[i], {"tp": peer})
        copy.start()
        sent.append(copy)
    start_pair(0)
    summed = piece_of(t)
    for copy in smalls[3:]:
        copy.wait()
    for m in range(pool_n * tp_n):
        gain_f[m : m + 1, :] = (
            gain_v[m * col : (m + 1) * col].astype(jnp.float32).reshape(1, col)
        )
    res = jnp.concatenate([res_v[b].astype(jnp.float32) for b in range(batches)], axis=0)
    summed = summed + res
    for i, peer in enumerate(z_to):
        send(
            part_s.at[i], part_r.at[i], part_ss.at[i], part_rs.at[i], {"tp": peer}
        ).wait_recv()
        summed = summed + part_r[i].astype(jnp.float32)
    hidden = summed.astype(jnp.bfloat16)
    hid[...] = hidden.astype(jnp.float32)
    hid_all[p, t] = hidden

    def hid_send(pp, tt, n, where):
        return send(
            hid_all.at[pp, tt], hid_all.at[pp, tt], hid_ss.at[n], hid_rs.at[pp, tt], where
        )

    for i, peer in enumerate(z_to):
        copy = hid_send(p, t, i, {"tp": peer})
        copy.start()
        sent.append(copy)
    order = [t] + z_from
    n = tp_n - 1
    for i, tt in enumerate(order):
        if i > 0:
            hid_send(p, tt, i - 1, {"tp": tt}).wait_recv()
        for mate in (p_y, p_c):
            copy = hid_send(p, tt, n, {"pool": mate})
            copy.start()
            sent.append(copy)
            n += 1

    def scaled(m):
        total = jnp.zeros((rows, col), jnp.float32)
        for tt in range(tp_n):
            h = hid_all[m, tt].astype(jnp.float32)
            total = total + h * h
            xn[m, :, tt * col : (tt + 1) * col] = (h * gain_f[pl.ds(m * tp_n + tt, 1), :]).astype(jnp.bfloat16)
        return total

    def product(m, j, which):
        k_rows = pl.ds(pl.multiple_of(m * pool_w, pool_w), pool_w)
        return jnp.dot(xn[m], slots[j, which, k_rows, :], preferred_element_type=jnp.float32)

    squares = scaled(p)

    @pl.loop(0, chunks)
    def _(j):
        in_copy(j).wait()
        for which in range(2):
            acc[j, which] = product(p, j, which)

    for tt in order:
        hid_send(p_y, tt, 0, {"pool": p_y}).wait_recv()
        copy = hid_send(p_y, tt, n, {"pool": p_c})
        copy.start()
        sent.append(copy)
        n += 1
    squares = squares + scaled(p_y)
    for tt in order:
        hid_send(p_c, tt, 0, {"pool": p_c}).wait_recv()
    squares = squares + scaled(p_c)
    for tt in order:
        hid_send(p_yc, tt, 0, {"pool": p_c}).wait_recv()
    squares = squares + scaled(p_yc)
    inv = lax.rsqrt(jnp.sum(squares, axis=1, keepdims=True) / (pool_n * pool_w) + 1e-05)
    logits = inv * sum(
        lax.dot_general(
            xn[m],
            router_v[:, m * pool_w : (m + 1) * pool_w],
            NT,
            preferred_element_type=jnp.float32,
        )
        for m in range(pool_n)
    )
    experts = router_v.shape[0]
    own = p // group_size
    lane = lax.broadcasted_iota(jnp.int32, (tokens, experts), 1)
    coeffs = []
    for b in range(batches):
        lb = logits[b * tokens : (b + 1) * tokens]
        id0 = ids_v[b, 0:1, :].reshape(tokens, 1)
        id1 = ids_v[b, 1:2, :].reshape(tokens, 1)
        l0 = jnp.sum(jnp.where(lane == id0, lb, 0.0), axis=1, keepdims=True)
        l1 = jnp.sum(jnp.where(lane == id1, lb, 0.0), axis=1, keepdims=True)
        coeffs.append(
            jnp.where(id0 == own, jax.nn.sigmoid(l0 - l1), 0.0)
            + jnp.where(id1 == own, jax.nn.sigmoid(l1 - l0), 0.0)
        )
    coeff = jnp.concatenate(coeffs, axis=0)

    def gate_up(j):
        gate, up = [
            inv * (acc[j, which] + sum(product(m, j, which) for m in mates)) for which in range(2)
        ]
        act[:, pl.ds(pl.multiple_of(j * CHUNK, CHUNK), CHUNK)] = (
            jax.nn.silu(gate) * up
        ).astype(jnp.bfloat16)

    for j in range(3):
        gate_up(j)
        start_pair(j + 1)

    @pl.loop(3, chunks)
    def _(j):
        gate_up(j)

    def mix_send(n, e, i, peer):
        k = (peer + tp_n - t) % tp_n
        return send(
            mix_s.at[n, e],
            mix_r.at[i, k],
            mix_ss.at[n, e],
            mix_rs.at[i, k],
            {"pool": targets[i], "tp": peer},
        )

    for n, (i, h) in enumerate(groups):
        parts = []
        for c in range(per_half):
            out_copy(n, c).wait()
            parts.append(
                jnp.dot(
                    act[...],
                    slots[places[n // 2], n % 2, c * ffl : (c + 1) * ffl, :],
                    preferred_element_type=jnp.float32,
                )
            )
        whole = jnp.concatenate(parts, axis=1) * coeff
        for e in range(2):
            piece = whole[:, e * col : (e + 1) * col]
            mix_s[n, e] = piece.astype(jnp.bfloat16)
            if n < len(groups) - 1:
                copy = mix_send(n, e, i, 2 * h + e)
                copy.start()
                sent.append(copy)
            else:
                att_rows[:, e * col : (e + 1) * col] = piece
    last = len(groups) - 1
    copy = mix_send(last, 1 - t % 2, pool_n - 1, t + 1 - 2 * (t % 2))
    copy.start()
    sent.append(copy)
    result = hid[...] + piece_of(t % 2)
    for k in range(tp_n):
        for i in range(pool_n):
            if i < pool_n - 1 or k > 0:
                pltpu.make_async_remote_copy(
                    src_ref=mix_r.at[i, k],
                    dst_ref=mix_r.at[i, k],
                    send_sem=mix_ss.at[0, 0],
                    recv_sem=mix_rs.at[i, k],
                    device_id={"pool": targets[i], "tp": (t + tp_n - k) % tp_n},
                    device_id_type=MESH,
                ).wait_recv()
                result = result + mix_r[i, k].astype(jnp.float32)
    for b in range(batches):
        out_ref[b] = result[b * tokens : (b + 1) * tokens].astype(jnp.bfloat16)
    for copy in sent:
        copy.wait_send()


def fused(
    queries,
    new_kv,
    kv_cache,
    cache_lengths,
    residual_in,
    out_weight,
    norm_gain,
    router_weight,
    expert_in,
    expert_out,
    expert_ids,
):
    batches, seqs, q_width = queries.shape
    tokens, col = residual_in.shape[1:]
    rows = batches * tokens
    kvl = new_kv.shape[3] // HD
    group_q = HQ // KVH
    model = norm_gain.shape[0]
    experts = router_weight.shape[1]
    ffl = expert_out.shape[1]
    ctx = kv_cache.shape[3]
    tp_n = 4
    heads = batches * seqs * kvl * 8
    half_w = tp_n * col // 2
    per_half = half_w // CHUNK
    chunks = ffl // CHUNK
    bf, f32 = jnp.bfloat16, jnp.float32
    dma = pltpu.SemaphoreType.DMA
    sizes = (batches, seqs, kvl, group_q, HD, tokens, 4 // experts)
    return pl.pallas_call(
        functools.partial(layer_kernel, sizes),
        out_shape=jax.ShapeDtypeStruct(residual_in.shape, bf),
        in_specs=[pl.BlockSpec(memory_space=pl.ANY)] * 11,
        out_specs=pl.BlockSpec(memory_space=pltpu.VMEM),
        scratch_shapes=[
            pltpu.SMEM((seqs, batches), jnp.int32),
            pltpu.VMEM(queries.shape, bf),
            pltpu.VMEM(new_kv.shape, bf),
            pltpu.VMEM(kv_cache.shape, bf),
            pltpu.VMEM(residual_in.shape, bf),
            pltpu.VMEM((model,), bf),
            pltpu.VMEM((experts, model), bf),
            pltpu.VMEM((batches, 2, tokens), jnp.int32),
            pltpu.VMEM((chunks + 1, 2, model, CHUNK), bf),
            pltpu.VMEM((8, q_width), f32),
            pltpu.VMEM((batches * seqs, 2, kvl * HD), f32),
            pltpu.VMEM((heads, HD), f32),
            pltpu.VMEM((heads, ctx), f32),
            pltpu.VMEM((heads, HD), f32),
            pltpu.VMEM((4, 8, q_width), bf),
            pltpu.VMEM((rows, q_width), f32),
            pltpu.VMEM((tp_n - 1, rows, col), bf),
            pltpu.VMEM((tp_n - 1, rows, col), bf),
            pltpu.VMEM((rows, col), f32),
            pltpu.VMEM((4, tp_n, rows, col), bf),
            pltpu.VMEM((4 * tp_n, col), f32),
            pltpu.VMEM((4, rows, tp_n * col), bf),
            pltpu.VMEM((chunks, 2, rows, CHUNK), f32),
            pltpu.VMEM((rows, ffl), bf),
            pltpu.VMEM((8, 2, rows, col), bf),
            pltpu.VMEM((4, tp_n, rows, col), bf),
            dma((7,)),
            dma,
            dma((tp_n * col // CHUNK,)),
            dma((chunks,)),
            dma((8, per_half)),
            dma((3,)),
            dma((3,)),
            dma((tp_n - 1,)),
            dma((tp_n - 1,)),
            dma((15,)),
            dma((4, tp_n)),
            dma((8, 2)),
            dma((4, tp_n)),
        ],
        compiler_params=pltpu.CompilerParams(
            collective_id=0, has_side_effects=True, vmem_limit_bytes=63 * 1024 * 1024
        ),
        cost_estimate=pl.CostEstimate(
            flops=6 * rows * model * ffl,
            bytes_accessed=6 * model * ffl + 2 * out_weight.size,
            transcendentals=0,
        ),
        name="layer",
    )(
        cache_lengths.T,
        queries,
        new_kv,
        kv_cache,
        residual_in,
        out_weight,
        norm_gain,
        router_weight.T,
        expert_in,
        expert_out,
        expert_ids.transpose(0, 2, 1),
    )


def body(*arrays):
    queries, new_kv, _, _, residual_in, _, norm_gain, router_weight, _, expert_out, _ = arrays
    ffl, model = expert_out.shape[1:]
    col = residual_in.shape[2]
    fits = (
        lax.axis_size("pool") == 4
        and lax.axis_size("tp") == 4
        and 4 % router_weight.shape[1] == 0
        and col % 128 == 0
        and (2 * col) % CHUNK == 0
        and ffl % CHUNK == 0
        and ffl // CHUNK >= 4
        and 4 * col // CHUNK * ffl == 2 * model
        and 4 * col // CHUNK * queries.shape[2] <= 2 * model
        and queries.shape[2] == 4 * col
        and queries.shape[0] * queries.shape[1] <= 8
        and residual_in.shape[1] % 8 == 0
    )
    return fused(*arrays) if fits else shards(*arrays)


def solution(mesh):
    return jax.shard_map(
        body,
        mesh=mesh,
        in_specs=(
            P(None, ("grp", "pool"), "tp"),
            P(None, ("grp", "pool"), None, "tp"),
            P(None, ("grp", "pool"), None, None, "tp"),
            P(None, ("grp", "pool")),
            P(None, "grp", ("pool", "tp")),
            P("tp", "pool"),
            P(),
            P(),
            P("pool", None, None, "tp"),
            P("pool", "tp", None),
            P(None, "grp", None),
        ),
        out_specs=P(None, "grp", ("pool", "tp")),
        check_vma=False,
    )
```

```python
import functools
import math

import jax
import jax.numpy as jnp
from jax import lax
from jax.experimental import pallas as pl
from jax.experimental.pallas import tpu as pltpu
from jax.sharding import PartitionSpec as P

HQ = 48
KVH = 8
HD = 128


def attend(query_rows, new_pairs, cache_rows, lengths):
    seq_count = query_rows.shape[0]
    kv_local = new_pairs.shape[-1] // HD
    group_q = HQ // KVH
    cache_len = cache_rows.shape[2]
    query_heads = query_rows.reshape(seq_count, kv_local, group_q, HD)
    key_rows = cache_rows[:, 0].reshape(seq_count, cache_len, kv_local, HD)
    value_rows = cache_rows[:, 1].reshape(seq_count, cache_len, kv_local, HD)
    new_keys = new_pairs[:, 0].reshape(seq_count, kv_local, HD)
    new_values = new_pairs[:, 1].reshape(seq_count, kv_local, HD)
    score_scale = 1.0 / math.sqrt(HD)
    old_scores = (
        jnp.einsum("sgqd,scgd->sgqc", query_heads, key_rows, preferred_element_type=jnp.float32)
        * score_scale
    )
    new_scores = (
        jnp.einsum("sgqd,sgd->sgq", query_heads, new_keys, preferred_element_type=jnp.float32)
        * score_scale
    )
    positions = jnp.arange(cache_len, dtype=jnp.int32)
    valid_mask = positions[None, :] < lengths[:, None]
    old_scores = jnp.where(valid_mask[:, None, None, :], old_scores, -jnp.inf)
    row_max = jnp.maximum(jnp.max(old_scores, axis=-1), new_scores)
    old_exp = jnp.exp(old_scores - row_max[..., None])
    new_exp = jnp.exp(new_scores - row_max)
    row_total = jnp.sum(old_exp, axis=-1) + new_exp
    old_probs = (old_exp / row_total[..., None]).astype(jnp.bfloat16)
    new_probs = (new_exp / row_total).astype(jnp.bfloat16)
    attended = jnp.einsum(
        "sgqc,scgd->sgqd", old_probs, value_rows, preferred_element_type=jnp.float32
    )
    attended = (
        attended
        + new_probs.astype(jnp.float32)[..., None] * new_values.astype(jnp.float32)[:, :, None, :]
    )
    return attended.reshape(seq_count, kv_local * group_q * HD).astype(jnp.bfloat16)


def shards(
    queries,
    new_kv,
    kv_cache,
    cache_lengths,
    residual_in,
    out_weight,
    norm_gain,
    router_weight,
    expert_in,
    expert_out,
    expert_ids,
):
    experts = router_weight.shape[1]
    pool_count = lax.axis_size("pool")
    tp_count = lax.axis_size("tp")
    group_size = pool_count // experts
    own_expert = lax.axis_index("pool") // group_size
    batches = queries.shape[0]
    token_count = residual_in.shape[1]
    col_width = residual_in.shape[2]
    capacity = 3 * token_count // 4
    slots_all = jnp.arange(experts * capacity, dtype=jnp.int32)
    expert_range = jnp.arange(experts, dtype=jnp.int32)
    self_hot = (expert_range == own_expert).astype(jnp.float32)
    gain_f = norm_gain.astype(jnp.float32)
    hiddens = []
    pick_tables = []
    own_tables = []
    buffer_rows = []
    other_slots = []
    for micro_batch in range(batches):
        attended = attend(
            queries[micro_batch],
            new_kv[micro_batch],
            kv_cache[micro_batch],
            cache_lengths[micro_batch],
        )
        heads_out = jnp.dot(
            lax.all_gather(attended, "pool", axis=0, tiled=True),
            out_weight,
            preferred_element_type=jnp.float32,
        )
        summed = lax.psum_scatter(
            heads_out.reshape(token_count, tp_count, col_width),
            "tp",
            scatter_dimension=1,
            tiled=True,
        )
        hidden = (
            residual_in[micro_batch].astype(jnp.float32) + summed.reshape(token_count, col_width)
        ).astype(jnp.bfloat16)
        hiddens.append(hidden)
        chosen_ids = expert_ids[micro_batch]
        id_hot = (chosen_ids[:, :, None] == expert_range[None, None, :]).astype(jnp.int32)
        chosen = jnp.sum(id_hot, axis=1)
        before = jnp.cumsum(chosen, axis=0) - chosen
        slot_index = jnp.sum(id_hot * before[:, None, :], axis=2)
        buffer_row = chosen_ids * capacity + slot_index
        buffer_rows.append(buffer_row)
        pick_table = jnp.any(buffer_row[None, :, :] == slots_all[:, None, None], axis=2).astype(
            jnp.bfloat16
        )
        pick_tables.append(pick_table)
        own_table = lax.dynamic_slice_in_dim(pick_table, own_expert * capacity, capacity, 0)
        own_tables.append(own_table)
        other_ids = jnp.where(chosen_ids[:, 0] == own_expert, chosen_ids[:, 1], chosen_ids[:, 0])
        other_hot = (other_ids[:, None] == expert_range[None, :]).astype(jnp.bfloat16)
        other_slots.append(jnp.dot(own_table, other_hot, preferred_element_type=jnp.float32))
    packed = jnp.concatenate(
        [
            jnp.dot(pick_tables[b], hiddens[b], preferred_element_type=jnp.bfloat16).reshape(
                experts, capacity, col_width
            )
            for b in range(batches)
        ],
        axis=1,
    )
    outgoing = jnp.repeat(packed, group_size * tp_count, axis=0)
    expert_rows = lax.all_to_all(outgoing, ("pool", "tp"), split_axis=0, concat_axis=2, tiled=True)[
        0
    ]
    rows_f = expert_rows.astype(jnp.float32)
    mean_sq = jnp.mean(rows_f * rows_f, axis=-1, keepdims=True)
    normed = (rows_f * lax.rsqrt(mean_sq + 1e-05) * gain_f).astype(jnp.bfloat16)
    logits = jnp.dot(normed, router_weight, preferred_element_type=jnp.float32)
    other_slot = jnp.concatenate(other_slots, axis=0)
    logit_self = jnp.sum(logits * self_hot[None, :], axis=1)
    logit_other = jnp.sum(logits * other_slot, axis=1)
    weight = jax.nn.sigmoid(logit_self - logit_other)
    gate_up = jnp.einsum("cd,kdf->kcf", normed, expert_in[0], preferred_element_type=jnp.float32)
    activated = (jax.nn.silu(gate_up[0]) * gate_up[1]).astype(jnp.bfloat16)
    partial_value = (
        jnp.dot(activated, expert_out[0], preferred_element_type=jnp.float32) * weight[:, None]
    )
    returned = lax.all_to_all(
        partial_value, ("pool", "tp"), split_axis=1, concat_axis=0, tiled=True
    )
    merged = jnp.sum(
        returned.reshape(experts, group_size * tp_count, batches, capacity, col_width), axis=1
    )
    results = []
    for micro_batch in range(batches):
        merged_batch = merged[:, micro_batch].reshape(experts * capacity, col_width)
        combined = jnp.sum(
            jnp.take(merged_batch, buffer_rows[micro_batch].reshape(-1), axis=0).reshape(
                token_count, 2, col_width
            ),
            axis=1,
        )
        results.append((hiddens[micro_batch].astype(jnp.float32) + combined).astype(jnp.bfloat16))
    return jnp.stack(results)


MESH = pl.DeviceIdType.MESH
CHUNK = 256
NT = (((1,), (1,)), ((), ()))


def layer_kernel(
    sizes,
    len_hbm,
    q_hbm,
    nkv_hbm,
    kv_hbm,
    res_hbm,
    wo_hbm,
    gain_hbm,
    router_hbm,
    win_hbm,
    wout_hbm,
    ids_hbm,
    out_ref,
    lengths,
    q_v,
    nkv_v,
    kv_v,
    res_v,
    gain_v,
    router_v,
    ids_v,
    slots,
    att,
    nkvf,
    qh,
    scores,
    newp,
    att_all,
    att_rows,
    part_s,
    part_r,
    hid,
    hid_all,
    gain_f,
    xn,
    acc,
    act,
    mix_s,
    mix_r,
    small_sem,
    kv_sem,
    wo_sem,
    in_sem,
    out_sem,
    att_ss,
    att_rs,
    part_ss,
    part_rs,
    hid_ss,
    hid_rs,
    mix_ss,
    mix_rs,
):
    batches, seqs, kvl, group_q, hd, tokens, group_size = sizes
    pool_n, tp_n = 4, 4
    rows = batches * tokens
    col = res_v.shape[2]
    ffl = wout_hbm.shape[1]
    chunks = win_hbm.shape[3] // CHUNK
    half_w = 2 * col
    per_half = half_w // CHUNK
    pool_w = tp_n * col

    p = lax.axis_index("pool")
    t = lax.axis_index("tp")
    flip = 1 - 2 * (p % 2)
    p_y = (p + 2) % 4
    p_c = p + flip
    p_yc = (p_y + flip) % 4
    mates = (p_y, p_yc, p_c)
    z_to = [(t + k) % tp_n for k in range(1, tp_n)]
    z_from = [(t + tp_n - k) % tp_n for k in range(1, tp_n)]

    barrier = pltpu.get_barrier_semaphore()
    targets = mates + (p,)
    others = [(m, z) for m in targets for z in z_to + [t]][:-1]
    for mate, peer in others:
        pl.semaphore_signal(
            barrier, inc=1, device_id={"pool": mate, "tp": peer}, device_id_type=MESH
        )

    smalls = [
        pltpu.make_async_copy(src, dst, small_sem.at[i])
        for i, (src, dst) in enumerate(
            [
                (q_hbm, q_v),
                (nkv_hbm, nkv_v),
                (len_hbm, lengths),
                (res_hbm, res_v),
                (gain_hbm, gain_v),
                (router_hbm, router_v),
                (ids_hbm, ids_v),
            ]
        )
    ]
    for copy in smalls[:3]:
        copy.start()
    kv_copy = pltpu.make_async_copy(kv_hbm, kv_v, kv_sem)
    kv_copy.start()
    for copy in smalls[3:]:
        copy.start()
    q_width = wo_hbm.shape[0]
    wide = 2 * CHUNK

    def wo_at(c):
        return slots.at[chunks, pl.ds(c * q_width, q_width), :]

    wo_copies = [
        pltpu.make_async_copy(wo_hbm.at[:, pl.ds(c * wide, wide)], wo_at(c), wo_sem.at[c])
        for c in range(pool_w // wide)
    ]
    for copy in wo_copies:
        copy.start()

    def in_copy(j, i, which):
        from_row = pl.multiple_of(targets[i] * pool_w, pool_w)
        return pltpu.make_async_copy(
            win_hbm.at[
                0, which, pl.ds(from_row, pool_w), pl.ds(pl.multiple_of(j * CHUNK, CHUNK), CHUNK)
            ],
            slots.at[j, pl.ds(i * pool_w, pool_w), pl.ds(which * CHUNK, CHUNK)],
            in_sem.at[j, i, which],
        )

    far, near = 1 - t // 2, t // 2
    groups = [(i, h) for h in (far, near) for i in range(pool_n)]
    places = [chunks, 0, 1, 2]

    def out_copy(n, c):
        start = targets[groups[n][0]] * pool_w + groups[n][1] * half_w + c * CHUNK
        return pltpu.make_async_copy(
            wout_hbm.at[0, :, pl.ds(pl.multiple_of(start, CHUNK), CHUNK)],
            slots.at[
                places[n // 2],
                pl.ds((n % 2 * per_half + c) // 2 * ffl, ffl),
                pl.ds((n % 2 * per_half + c) % 2 * CHUNK, CHUNK),
            ],
            out_sem.at[n, c],
        )

    def start_pair(pair):
        for n in (2 * pair, 2 * pair + 1):
            for c in range(per_half):
                out_copy(n, c).start()

    for copy in smalls[:3]:
        copy.wait()
    qh[...] = jnp.zeros_like(qh)
    for b in range(batches):
        att[pl.ds(b * seqs, seqs), :] = q_v[b].astype(jnp.float32)
    for b in range(batches):
        for s in range(seqs):
            nkvf[b * seqs + s] = nkv_v[b, s].astype(jnp.float32)
    for r in range(batches * seqs):
        for g in range(kvl):
            for h in range(group_q):
                qh[pl.ds((r * kvl + g) * 8 + h, 1), :] = att[
                    pl.ds(r, 1), pl.ds((g * group_q + h) * hd, hd)
                ]
    att[...] = jnp.zeros_like(att)
    kv_copy.wait()

    @pl.loop(0, chunks)
    def _(j):
        for i in range(pool_n):
            for which in range(2):
                in_copy(j, i, which).start()
    ctx = kv_v.shape[3]
    scale = 1.0 / math.sqrt(hd)
    place = lax.broadcasted_iota(jnp.int32, (8, ctx), 1)
    news = []
    for r in range(batches * seqs):
        b, s = r // seqs, r % seqs
        for g in range(kvl):
            q8 = qh[pl.ds((r * kvl + g) * 8, 8), :]
            keys = kv_v[b, s, 0, :, g * hd : (g + 1) * hd]
            sc = (
                lax.dot_general(
                    q8.astype(jnp.bfloat16), keys, NT, preferred_element_type=jnp.float32
                )
                * scale
            )
            scores[pl.ds((r * kvl + g) * 8, 8), :] = jnp.where(
                place < lengths[s, b], sc, -jnp.inf
            )
            nk = nkvf[r, 0:1, g * hd : (g + 1) * hd]
            news.append(jnp.sum(q8 * nk, axis=1, keepdims=True) * scale)
    new = jnp.concatenate(news, axis=0)
    old = scores[...]
    top = jnp.maximum(jnp.max(old, axis=1, keepdims=True), new)
    old_exp = jnp.exp(old - top)
    new_exp = jnp.exp(new - top)
    total = jnp.sum(old_exp, axis=1, keepdims=True) + new_exp
    scores[...] = old_exp / total
    newp[...] = jnp.broadcast_to(
        (new_exp / total).astype(jnp.bfloat16).astype(jnp.float32), newp.shape
    )
    for r in range(batches * seqs):
        b, s = r // seqs, r % seqs
        for g in range(kvl):
            at = pl.ds((r * kvl + g) * 8, 8)
            values = kv_v[b, s, 1, :, g * hd : (g + 1) * hd]
            o8 = jnp.dot(
                scores[at, :].astype(jnp.bfloat16), values, preferred_element_type=jnp.float32
            )
            o8 = o8 + newp[at, :] * nkvf[r, 1:2, g * hd : (g + 1) * hd]
            for h in range(group_q):
                att[r : r + 1, (g * group_q + h) * hd : (g * group_q + h + 1) * hd] = o8[h : h + 1]
    att_all[p] = att[...].astype(jnp.bfloat16)

    pl.semaphore_wait(barrier, len(others))

    def send(src, dst, ss, rs, where):
        return pltpu.make_async_remote_copy(
            src_ref=src, dst_ref=dst, send_sem=ss, recv_sem=rs, device_id=where,
            device_id_type=MESH,
        )

    sent = []
    att_copies = []
    for i, mate in enumerate(mates):
        copy = send(att_all.at[p], att_all.at[p], att_ss.at[i], att_rs.at[i], {"pool": mate})
        copy.start()
        att_copies.append(copy)
    for copy in wo_copies:
        copy.wait()
    for i, mate in enumerate(mates):
        send(
            att_all.at[mate], att_all.at[mate], att_ss.at[i], att_rs.at[i], {"pool": mate}
        ).wait_recv()
    sent += att_copies
    for m in range(pool_n):
        x = att_all[m].astype(jnp.float32)
        for b in range(batches):
            att_rows[pl.ds(b * tokens + m * seqs, seqs), :] = x[b * seqs : (b + 1) * seqs]
    lhs = att_rows[...].astype(jnp.bfloat16)

    for c in range(pool_w // wide):
        att_rows[:, c * wide : (c + 1) * wide] = jnp.dot(
            lhs, wo_at(c)[...], preferred_element_type=jnp.float32
        )

    def piece_of(who):
        return att_rows[:, pl.ds(pl.multiple_of(who * col, col), col)]

    for i, peer in enumerate(z_to):
        part_s[i] = piece_of(peer).astype(jnp.bfloat16)
        copy = send(part_s.at[i], part_r.at[i], part_ss.at[i], part_rs.at[i], {"tp": peer})
        copy.start()
        sent.append(copy)
    start_pair(0)
    summed = piece_of(t)
    for copy in smalls[3:]:
        copy.wait()
    for m in range(pool_n * tp_n):
        gain_f[m : m + 1, :] = (
            gain_v[m * col : (m + 1) * col].astype(jnp.float32).reshape(1, col)
        )
    res = jnp.concatenate([res_v[b].astype(jnp.float32) for b in range(batches)], axis=0)
    summed = summed + res
    for i, peer in enumerate(z_to):
        send(
            part_s.at[i], part_r.at[i], part_ss.at[i], part_rs.at[i], {"tp": peer}
        ).wait_recv()
        summed = summed + part_r[i].astype(jnp.float32)
    hidden = summed.astype(jnp.bfloat16)
    hid[...] = hidden.astype(jnp.float32)
    hid_all[p, t] = hidden

    def hid_send(pp, tt, n, where):
        return send(
            hid_all.at[pp, tt], hid_all.at[pp, tt], hid_ss.at[n], hid_rs.at[pp, tt], where
        )

    for i, peer in enumerate(z_to):
        copy = hid_send(p, t, i, {"tp": peer})
        copy.start()
        sent.append(copy)
    order = [t] + z_from
    n = tp_n - 1
    for i, tt in enumerate(order):
        if i > 0:
            hid_send(p, tt, i - 1, {"tp": tt}).wait_recv()
        for mate in (p_y, p_c):
            copy = hid_send(p, tt, n, {"pool": mate})
            copy.start()
            sent.append(copy)
            n += 1

    def scaled(i):
        m = targets[i]
        total = jnp.zeros((rows, col), jnp.float32)
        for tt in range(tp_n):
            h = hid_all[m, tt].astype(jnp.float32)
            total = total + h * h
            xn[:, i * pool_w + tt * col : i * pool_w + (tt + 1) * col] = (
                h * gain_f[pl.ds(m * tp_n + tt, 1), :]
            ).astype(jnp.bfloat16)
        return total

    squares = scaled(pool_n - 1)
    cut = (pool_n - 1) * pool_w

    @pl.loop(0, chunks)
    def _(j):
        for which in range(2):
            in_copy(j, pool_n - 1, which).wait()
        acc[j] = jnp.dot(xn[:, cut:], slots[j, cut:, :], preferred_element_type=jnp.float32)

    for tt in order:
        hid_send(p_y, tt, 0, {"pool": p_y}).wait_recv()
        copy = hid_send(p_y, tt, n, {"pool": p_c})
        copy.start()
        sent.append(copy)
        n += 1
    squares = squares + scaled(0)
    for tt in order:
        hid_send(p_c, tt, 0, {"pool": p_c}).wait_recv()
    squares = squares + scaled(2)
    for tt in order:
        hid_send(p_yc, tt, 0, {"pool": p_c}).wait_recv()
    squares = squares + scaled(1)
    inv = lax.rsqrt(jnp.sum(squares, axis=1, keepdims=True) / (pool_n * pool_w) + 1e-05)
    logits = inv * sum(
        lax.dot_general(
            xn[:, i * pool_w : (i + 1) * pool_w],
            router_v[:, pl.ds(pl.multiple_of(m * pool_w, pool_w), pool_w)],
            NT,
            preferred_element_type=jnp.float32,
        )
        for i, m in enumerate(targets)
    )
    experts = router_v.shape[0]
    own = p // group_size
    lane = lax.broadcasted_iota(jnp.int32, (tokens, experts), 1)
    coeffs = []
    for b in range(batches):
        lb = logits[b * tokens : (b + 1) * tokens]
        id0 = ids_v[b, 0:1, :].reshape(tokens, 1)
        id1 = ids_v[b, 1:2, :].reshape(tokens, 1)
        l0 = jnp.sum(jnp.where(lane == id0, lb, 0.0), axis=1, keepdims=True)
        l1 = jnp.sum(jnp.where(lane == id1, lb, 0.0), axis=1, keepdims=True)
        coeffs.append(
            jnp.where(id0 == own, jax.nn.sigmoid(l0 - l1), 0.0)
            + jnp.where(id1 == own, jax.nn.sigmoid(l1 - l0), 0.0)
        )
    coeff = jnp.concatenate(coeffs, axis=0)

    def gate_up(j):
        for i in range(pool_n - 1):
            for which in range(2):
                in_copy(j, i, which).wait()
        both = inv * (
            acc[j]
            + jnp.dot(xn[:, :cut], slots[j, :cut, :], preferred_element_type=jnp.float32)
        )
        gate, up = both[:, :CHUNK], both[:, CHUNK:]
        act[:, pl.ds(pl.multiple_of(j * CHUNK, CHUNK), CHUNK)] = (
            jax.nn.silu(gate) * up
        ).astype(jnp.bfloat16)

    for j in range(3):
        gate_up(j)
        start_pair(j + 1)

    @pl.loop(3, chunks)
    def _(j):
        gate_up(j)

    def mix_send(n, e, i, peer):
        k = (peer + tp_n - t) % tp_n
        return send(
            mix_s.at[n, e],
            mix_r.at[i, k],
            mix_ss.at[n, e],
            mix_rs.at[i, k],
            {"pool": targets[i], "tp": peer},
        )

    def down(pair, c):
        return jnp.dot(
            act[...],
            slots[places[pair], c * ffl : (c + 1) * ffl, :],
            preferred_element_type=jnp.float32,
        )

    for n, (i, h) in enumerate(groups):
        for c in range(n % 2, per_half):
            out_copy(n, c).wait()
        if n % 2 == 0:
            out_copy(n + 1, 0).wait()
            out_cols = [down(n // 2, 0), down(n // 2, 1)]
            whole = jnp.concatenate([out_cols[0], out_cols[1][:, :CHUNK]], axis=1) * coeff
        else:
            whole = (
                jnp.concatenate([out_cols[1][:, CHUNK:], down(n // 2, 2)], axis=1) * coeff
            )
        for e in range(2):
            piece = whole[:, e * col : (e + 1) * col]
            mix_s[n, e] = piece.astype(jnp.bfloat16)
            if n < len(groups) - 1:
                copy = mix_send(n, e, i, 2 * h + e)
                copy.start()
                sent.append(copy)
            else:
                att_rows[:, e * col : (e + 1) * col] = piece
    last = len(groups) - 1
    copy = mix_send(last, 1 - t % 2, pool_n - 1, t + 1 - 2 * (t % 2))
    copy.start()
    sent.append(copy)
    result = hid[...] + piece_of(t % 2)
    for k in range(tp_n):
        for i in range(pool_n):
            if i < pool_n - 1 or k > 0:
                pltpu.make_async_remote_copy(
                    src_ref=mix_r.at[i, k],
                    dst_ref=mix_r.at[i, k],
                    send_sem=mix_ss.at[0, 0],
                    recv_sem=mix_rs.at[i, k],
                    device_id={"pool": targets[i], "tp": (t + tp_n - k) % tp_n},
                    device_id_type=MESH,
                ).wait_recv()
                result = result + mix_r[i, k].astype(jnp.float32)
    for b in range(batches):
        out_ref[b] = result[b * tokens : (b + 1) * tokens].astype(jnp.bfloat16)
    for copy in sent:
        copy.wait_send()


def fused(
    queries,
    new_kv,
    kv_cache,
    cache_lengths,
    residual_in,
    out_weight,
    norm_gain,
    router_weight,
    expert_in,
    expert_out,
    expert_ids,
):
    batches, seqs, q_width = queries.shape
    tokens, col = residual_in.shape[1:]
    rows = batches * tokens
    kvl = new_kv.shape[3] // HD
    group_q = HQ // KVH
    model = norm_gain.shape[0]
    experts = router_weight.shape[1]
    ffl = expert_out.shape[1]
    ctx = kv_cache.shape[3]
    tp_n = 4
    heads = batches * seqs * kvl * 8
    half_w = tp_n * col // 2
    per_half = half_w // CHUNK
    chunks = ffl // CHUNK
    bf, f32 = jnp.bfloat16, jnp.float32
    dma = pltpu.SemaphoreType.DMA
    sizes = (batches, seqs, kvl, group_q, HD, tokens, 4 // experts)
    return pl.pallas_call(
        functools.partial(layer_kernel, sizes),
        out_shape=jax.ShapeDtypeStruct(residual_in.shape, bf),
        in_specs=[pl.BlockSpec(memory_space=pl.ANY)] * 11,
        out_specs=pl.BlockSpec(memory_space=pltpu.VMEM),
        scratch_shapes=[
            pltpu.SMEM((seqs, batches), jnp.int32),
            pltpu.VMEM(queries.shape, bf),
            pltpu.VMEM(new_kv.shape, bf),
            pltpu.VMEM(kv_cache.shape, bf),
            pltpu.VMEM(residual_in.shape, bf),
            pltpu.VMEM((model,), bf),
            pltpu.VMEM((experts, model), bf),
            pltpu.VMEM((batches, 2, tokens), jnp.int32),
            pltpu.VMEM((chunks + 1, model, 2 * CHUNK), bf),
            pltpu.VMEM((8, q_width), f32),
            pltpu.VMEM((batches * seqs, 2, kvl * HD), f32),
            pltpu.VMEM((heads, HD), f32),
            pltpu.VMEM((heads, ctx), f32),
            pltpu.VMEM((heads, HD), f32),
            pltpu.VMEM((4, 8, q_width), bf),
            pltpu.VMEM((rows, q_width), f32),
            pltpu.VMEM((tp_n - 1, rows, col), bf),
            pltpu.VMEM((tp_n - 1, rows, col), bf),
            pltpu.VMEM((rows, col), f32),
            pltpu.VMEM((4, tp_n, rows, col), bf),
            pltpu.VMEM((4 * tp_n, col), f32),
            pltpu.VMEM((rows, model), bf),
            pltpu.VMEM((chunks, rows, 2 * CHUNK), f32),
            pltpu.VMEM((rows, ffl), bf),
            pltpu.VMEM((8, 2, rows, col), bf),
            pltpu.VMEM((4, tp_n, rows, col), bf),
            dma((7,)),
            dma,
            dma((tp_n * col // (2 * CHUNK),)),
            dma((chunks, 4, 2)),
            dma((8, per_half)),
            dma((3,)),
            dma((3,)),
            dma((tp_n - 1,)),
            dma((tp_n - 1,)),
            dma((15,)),
            dma((4, tp_n)),
            dma((8, 2)),
            dma((4, tp_n)),
        ],
        compiler_params=pltpu.CompilerParams(
            collective_id=0, has_side_effects=True, vmem_limit_bytes=63 * 1024 * 1024
        ),
        cost_estimate=pl.CostEstimate(
            flops=6 * rows * model * ffl,
            bytes_accessed=6 * model * ffl + 2 * out_weight.size,
            transcendentals=0,
        ),
        name="layer",
    )(
        cache_lengths.T,
        queries,
        new_kv,
        kv_cache,
        residual_in,
        out_weight,
        norm_gain,
        router_weight.T,
        expert_in,
        expert_out,
        expert_ids.transpose(0, 2, 1),
    )


def body(*arrays):
    queries, new_kv, _, _, residual_in, _, norm_gain, router_weight, _, expert_out, _ = arrays
    ffl, model = expert_out.shape[1:]
    col = residual_in.shape[2]
    fits = (
        lax.axis_size("pool") == 4
        and lax.axis_size("tp") == 4
        and 4 % router_weight.shape[1] == 0
        and col % 128 == 0
        and 2 * col == 3 * CHUNK
        and ffl % CHUNK == 0
        and ffl // CHUNK >= 4
        and 4 * col // CHUNK * ffl == 2 * model
        and queries.shape[2] == 4 * col
        and queries.shape[0] * queries.shape[1] <= 8
        and residual_in.shape[1] % 8 == 0
    )
    return fused(*arrays) if fits else shards(*arrays)


def solution(mesh):
    return jax.shard_map(
        body,
        mesh=mesh,
        in_specs=(
            P(None, ("grp", "pool"), "tp"),
            P(None, ("grp", "pool"), None, "tp"),
            P(None, ("grp", "pool"), None, None, "tp"),
            P(None, ("grp", "pool")),
            P(None, "grp", ("pool", "tp")),
            P("tp", "pool"),
            P(),
            P(),
            P("pool", None, None, "tp"),
            P("pool", "tp", None),
            P(None, "grp", None),
        ),
        out_specs=P(None, "grp", ("pool", "tp")),
        check_vma=False,
    )
```

```python
import functools
import math

import jax
import jax.numpy as jnp
from jax import lax
from jax.experimental import pallas as pl
from jax.experimental.pallas import tpu as pltpu
from jax.sharding import PartitionSpec as P

HQ = 48
KVH = 8
HD = 128


def attend(query_rows, new_pairs, cache_rows, lengths):
    seq_count = query_rows.shape[0]
    kv_local = new_pairs.shape[-1] // HD
    group_q = HQ // KVH
    cache_len = cache_rows.shape[2]
    query_heads = query_rows.reshape(seq_count, kv_local, group_q, HD)
    key_rows = cache_rows[:, 0].reshape(seq_count, cache_len, kv_local, HD)
    value_rows = cache_rows[:, 1].reshape(seq_count, cache_len, kv_local, HD)
    new_keys = new_pairs[:, 0].reshape(seq_count, kv_local, HD)
    new_values = new_pairs[:, 1].reshape(seq_count, kv_local, HD)
    score_scale = 1.0 / math.sqrt(HD)
    old_scores = (
        jnp.einsum("sgqd,scgd->sgqc", query_heads, key_rows, preferred_element_type=jnp.float32)
        * score_scale
    )
    new_scores = (
        jnp.einsum("sgqd,sgd->sgq", query_heads, new_keys, preferred_element_type=jnp.float32)
        * score_scale
    )
    positions = jnp.arange(cache_len, dtype=jnp.int32)
    valid_mask = positions[None, :] < lengths[:, None]
    old_scores = jnp.where(valid_mask[:, None, None, :], old_scores, -jnp.inf)
    row_max = jnp.maximum(jnp.max(old_scores, axis=-1), new_scores)
    old_exp = jnp.exp(old_scores - row_max[..., None])
    new_exp = jnp.exp(new_scores - row_max)
    row_total = jnp.sum(old_exp, axis=-1) + new_exp
    old_probs = (old_exp / row_total[..., None]).astype(jnp.bfloat16)
    new_probs = (new_exp / row_total).astype(jnp.bfloat16)
    attended = jnp.einsum(
        "sgqc,scgd->sgqd", old_probs, value_rows, preferred_element_type=jnp.float32
    )
    attended = (
        attended
        + new_probs.astype(jnp.float32)[..., None] * new_values.astype(jnp.float32)[:, :, None, :]
    )
    return attended.reshape(seq_count, kv_local * group_q * HD).astype(jnp.bfloat16)


def shards(
    queries,
    new_kv,
    kv_cache,
    cache_lengths,
    residual_in,
    out_weight,
    norm_gain,
    router_weight,
    expert_in,
    expert_out,
    expert_ids,
):
    experts = router_weight.shape[1]
    pool_count = lax.axis_size("pool")
    tp_count = lax.axis_size("tp")
    group_size = pool_count // experts
    own_expert = lax.axis_index("pool") // group_size
    batches = queries.shape[0]
    token_count = residual_in.shape[1]
    col_width = residual_in.shape[2]
    capacity = 3 * token_count // 4
    slots_all = jnp.arange(experts * capacity, dtype=jnp.int32)
    expert_range = jnp.arange(experts, dtype=jnp.int32)
    self_hot = (expert_range == own_expert).astype(jnp.float32)
    gain_f = norm_gain.astype(jnp.float32)
    hiddens = []
    pick_tables = []
    own_tables = []
    buffer_rows = []
    other_slots = []
    for micro_batch in range(batches):
        attended = attend(
            queries[micro_batch],
            new_kv[micro_batch],
            kv_cache[micro_batch],
            cache_lengths[micro_batch],
        )
        heads_out = jnp.dot(
            lax.all_gather(attended, "pool", axis=0, tiled=True),
            out_weight,
            preferred_element_type=jnp.float32,
        )
        summed = lax.psum_scatter(
            heads_out.reshape(token_count, tp_count, col_width),
            "tp",
            scatter_dimension=1,
            tiled=True,
        )
        hidden = (
            residual_in[micro_batch].astype(jnp.float32) + summed.reshape(token_count, col_width)
        ).astype(jnp.bfloat16)
        hiddens.append(hidden)
        chosen_ids = expert_ids[micro_batch]
        id_hot = (chosen_ids[:, :, None] == expert_range[None, None, :]).astype(jnp.int32)
        chosen = jnp.sum(id_hot, axis=1)
        before = jnp.cumsum(chosen, axis=0) - chosen
        slot_index = jnp.sum(id_hot * before[:, None, :], axis=2)
        buffer_row = chosen_ids * capacity + slot_index
        buffer_rows.append(buffer_row)
        pick_table = jnp.any(buffer_row[None, :, :] == slots_all[:, None, None], axis=2).astype(
            jnp.bfloat16
        )
        pick_tables.append(pick_table)
        own_table = lax.dynamic_slice_in_dim(pick_table, own_expert * capacity, capacity, 0)
        own_tables.append(own_table)
        other_ids = jnp.where(chosen_ids[:, 0] == own_expert, chosen_ids[:, 1], chosen_ids[:, 0])
        other_hot = (other_ids[:, None] == expert_range[None, :]).astype(jnp.bfloat16)
        other_slots.append(jnp.dot(own_table, other_hot, preferred_element_type=jnp.float32))
    packed = jnp.concatenate(
        [
            jnp.dot(pick_tables[b], hiddens[b], preferred_element_type=jnp.bfloat16).reshape(
                experts, capacity, col_width
            )
            for b in range(batches)
        ],
        axis=1,
    )
    outgoing = jnp.repeat(packed, group_size * tp_count, axis=0)
    expert_rows = lax.all_to_all(outgoing, ("pool", "tp"), split_axis=0, concat_axis=2, tiled=True)[
        0
    ]
    rows_f = expert_rows.astype(jnp.float32)
    mean_sq = jnp.mean(rows_f * rows_f, axis=-1, keepdims=True)
    normed = (rows_f * lax.rsqrt(mean_sq + 1e-05) * gain_f).astype(jnp.bfloat16)
    logits = jnp.dot(normed, router_weight, preferred_element_type=jnp.float32)
    other_slot = jnp.concatenate(other_slots, axis=0)
    logit_self = jnp.sum(logits * self_hot[None, :], axis=1)
    logit_other = jnp.sum(logits * other_slot, axis=1)
    weight = jax.nn.sigmoid(logit_self - logit_other)
    gate_up = jnp.einsum("cd,kdf->kcf", normed, expert_in[0], preferred_element_type=jnp.float32)
    activated = (jax.nn.silu(gate_up[0]) * gate_up[1]).astype(jnp.bfloat16)
    partial_value = (
        jnp.dot(activated, expert_out[0], preferred_element_type=jnp.float32) * weight[:, None]
    )
    returned = lax.all_to_all(
        partial_value, ("pool", "tp"), split_axis=1, concat_axis=0, tiled=True
    )
    merged = jnp.sum(
        returned.reshape(experts, group_size * tp_count, batches, capacity, col_width), axis=1
    )
    results = []
    for micro_batch in range(batches):
        merged_batch = merged[:, micro_batch].reshape(experts * capacity, col_width)
        combined = jnp.sum(
            jnp.take(merged_batch, buffer_rows[micro_batch].reshape(-1), axis=0).reshape(
                token_count, 2, col_width
            ),
            axis=1,
        )
        results.append((hiddens[micro_batch].astype(jnp.float32) + combined).astype(jnp.bfloat16))
    return jnp.stack(results)


MESH = pl.DeviceIdType.MESH
CHUNK = 256
NT = (((1,), (1,)), ((), ()))


def layer_kernel(
    sizes,
    len_hbm,
    q_hbm,
    nkv_hbm,
    kv_hbm,
    res_hbm,
    wo_hbm,
    gain_hbm,
    router_hbm,
    win_hbm,
    wout_hbm,
    ids_hbm,
    out_ref,
    lengths,
    q_v,
    nkv_v,
    kv_v,
    res_v,
    gain_v,
    router_v,
    ids_v,
    slots,
    att,
    nkvf,
    qh,
    scores,
    newp,
    att_all,
    att_rows,
    part_s,
    part_r,
    hid,
    hid_all,
    gain_f,
    xn,
    acc,
    act,
    mix_s,
    mix_r,
    small_sem,
    kv_sem,
    wo_sem,
    in_sem,
    out_sem,
    att_ss,
    att_rs,
    part_ss,
    part_rs,
    hid_ss,
    hid_rs,
    mix_ss,
    mix_rs,
):
    batches, seqs, kvl, group_q, hd, tokens, group_size = sizes
    pool_n, tp_n = 4, 4
    rows = batches * tokens
    col = res_v.shape[2]
    ffl = wout_hbm.shape[1]
    chunks = win_hbm.shape[3] // CHUNK
    half_w = 2 * col
    per_half = half_w // CHUNK
    pool_w = tp_n * col

    p = lax.axis_index("pool")
    t = lax.axis_index("tp")
    flip = 1 - 2 * (p % 2)
    p_y = (p + 2) % 4
    p_c = p + flip
    p_yc = (p_y + flip) % 4
    mates = (p_y, p_yc, p_c)
    z_to = [(t + k) % tp_n for k in range(1, tp_n)]
    z_from = [(t + tp_n - k) % tp_n for k in range(1, tp_n)]

    barrier = pltpu.get_barrier_semaphore()
    targets = mates + (p,)
    others = [(m, z) for m in targets for z in z_to + [t]][:-1]
    for mate, peer in others:
        pl.semaphore_signal(
            barrier, inc=1, device_id={"pool": mate, "tp": peer}, device_id_type=MESH
        )

    smalls = [
        pltpu.make_async_copy(src, dst, small_sem.at[i])
        for i, (src, dst) in enumerate(
            [
                (q_hbm, q_v),
                (nkv_hbm, nkv_v),
                (len_hbm, lengths),
                (res_hbm, res_v),
                (gain_hbm, gain_v),
                (router_hbm, router_v),
                (ids_hbm, ids_v),
            ]
        )
    ]
    for copy in smalls[:3]:
        copy.start()
    kv_copy = pltpu.make_async_copy(kv_hbm, kv_v, kv_sem)
    kv_copy.start()
    for copy in smalls[3:]:
        copy.start()
    q_width = wo_hbm.shape[0]
    stack = slots.shape[2] // q_width

    def wo_at(c):
        return slots.at[chunks, c // stack, pl.ds(c % stack * q_width, q_width), :]

    wo_copies = [
        pltpu.make_async_copy(wo_hbm.at[:, pl.ds(c * CHUNK, CHUNK)], wo_at(c), wo_sem.at[c])
        for c in range(pool_w // CHUNK)
    ]
    for copy in wo_copies:
        copy.start()

    def in_copy(j):
        return pltpu.make_async_copy(
            win_hbm.at[0, :, :, pl.ds(pl.multiple_of(j * CHUNK, CHUNK), CHUNK)],
            slots.at[j],
            in_sem.at[j],
        )

    far, near = 1 - t // 2, t // 2
    groups = [(i, h) for h in (far, near) for i in range(pool_n)]
    places = [chunks, 0, 1, 2]

    def out_copy(n, c):
        start = targets[groups[n][0]] * pool_w + groups[n][1] * half_w + c * CHUNK
        return pltpu.make_async_copy(
            wout_hbm.at[0, :, pl.ds(pl.multiple_of(start, CHUNK), CHUNK)],
            slots.at[places[n // 2], n % 2, pl.ds(c * ffl, ffl), :],
            out_sem.at[n, c],
        )

    def start_pair(pair):
        for n in (2 * pair, 2 * pair + 1):
            for c in range(per_half):
                out_copy(n, c).start()

    for copy in smalls[:3]:
        copy.wait()
    qh[...] = jnp.zeros_like(qh)
    for b in range(batches):
        att[pl.ds(b * seqs, seqs), :] = q_v[b].astype(jnp.float32)
    for b in range(batches):
        for s in range(seqs):
            nkvf[b * seqs + s] = nkv_v[b, s].astype(jnp.float32)
    for r in range(batches * seqs):
        for g in range(kvl):
            for h in range(group_q):
                qh[pl.ds((r * kvl + g) * 8 + h, 1), :] = att[
                    pl.ds(r, 1), pl.ds((g * group_q + h) * hd, hd)
                ]
    att[...] = jnp.zeros_like(att)
    kv_copy.wait()

    @pl.loop(0, chunks)
    def _(j):
        in_copy(j).start()
    ctx = kv_v.shape[3]
    scale = 1.0 / math.sqrt(hd)
    place = lax.broadcasted_iota(jnp.int32, (8, ctx), 1)
    news = []
    for r in range(batches * seqs):
        b, s = r // seqs, r % seqs
        for g in range(kvl):
            q8 = qh[pl.ds((r * kvl + g) * 8, 8), :]
            keys = kv_v[b, s, 0, :, g * hd : (g + 1) * hd]
            sc = (
                lax.dot_general(
                    q8.astype(jnp.bfloat16), keys, NT, preferred_element_type=jnp.float32
                )
                * scale
            )
            scores[pl.ds((r * kvl + g) * 8, 8), :] = jnp.where(
                place < lengths[s, b], sc, -jnp.inf
            )
            nk = nkvf[r, 0:1, g * hd : (g + 1) * hd]
            news.append(jnp.sum(q8 * nk, axis=1, keepdims=True) * scale)
    new = jnp.concatenate(news, axis=0)
    old = scores[...]
    top = jnp.maximum(jnp.max(old, axis=1, keepdims=True), new)
    old_exp = jnp.exp(old - top)
    new_exp = jnp.exp(new - top)
    total = jnp.sum(old_exp, axis=1, keepdims=True) + new_exp
    scores[...] = old_exp / total
    newp[...] = jnp.broadcast_to(
        (new_exp / total).astype(jnp.bfloat16).astype(jnp.float32), newp.shape
    )
    for r in range(batches * seqs):
        b, s = r // seqs, r % seqs
        for g in range(kvl):
            at = pl.ds((r * kvl + g) * 8, 8)
            values = kv_v[b, s, 1, :, g * hd : (g + 1) * hd]
            o8 = jnp.dot(
                scores[at, :].astype(jnp.bfloat16), values, preferred_element_type=jnp.float32
            )
            o8 = o8 + newp[at, :] * nkvf[r, 1:2, g * hd : (g + 1) * hd]
            for h in range(group_q):
                att[r : r + 1, (g * group_q + h) * hd : (g * group_q + h + 1) * hd] = o8[h : h + 1]
    att_all[p] = att[...].astype(jnp.bfloat16)

    pl.semaphore_wait(barrier, len(others))

    def send(src, dst, ss, rs, where):
        return pltpu.make_async_remote_copy(
            src_ref=src, dst_ref=dst, send_sem=ss, recv_sem=rs, device_id=where,
            device_id_type=MESH,
        )

    sent = []
    att_copies = []
    for i, mate in enumerate(mates):
        copy = send(att_all.at[p], att_all.at[p], att_ss.at[i], att_rs.at[i], {"pool": mate})
        copy.start()
        att_copies.append(copy)
    for copy in wo_copies:
        copy.wait()
    for i, mate in enumerate(mates):
        send(
            att_all.at[mate], att_all.at[mate], att_ss.at[i], att_rs.at[i], {"pool": mate}
        ).wait_recv()
    sent += att_copies
    for m in range(pool_n):
        x = att_all[m].astype(jnp.float32)
        for b in range(batches):
            att_rows[pl.ds(b * tokens + m * seqs, seqs), :] = x[b * seqs : (b + 1) * seqs]
    lhs = att_rows[...].astype(jnp.bfloat16)

    for c in range(pool_w // CHUNK):
        att_rows[:, c * CHUNK : (c + 1) * CHUNK] = jnp.dot(
            lhs, wo_at(c)[...], preferred_element_type=jnp.float32
        )

    def piece_of(who):
        return att_rows[:, pl.ds(pl.multiple_of(who * col, col), col)]

    for i, peer in enumerate(z_to):
        part_s[i] = piece_of(peer).astype(jnp.bfloat16)
        copy = send(part_s.at[i], part_r.at[i], part_ss.at[i], part_rs.at[i], {"tp": peer})
        copy.start()
        sent.append(copy)
    start_pair(0)
    summed = piece_of(t)
    for copy in smalls[3:]:
        copy.wait()
    for m in range(pool_n * tp_n):
        gain_f[m : m + 1, :] = (
            gain_v[m * col : (m + 1) * col].astype(jnp.float32).reshape(1, col)
        )
    res = jnp.concatenate([res_v[b].astype(jnp.float32) for b in range(batches)], axis=0)
    summed = summed + res
    for i, peer in enumerate(z_to):
        send(
            part_s.at[i], part_r.at[i], part_ss.at[i], part_rs.at[i], {"tp": peer}
        ).wait_recv()
        summed = summed + part_r[i].astype(jnp.float32)
    hidden = summed.astype(jnp.bfloat16)
    hid[...] = hidden.astype(jnp.float32)
    hid_all[p, t] = hidden

    def hid_send(pp, tt, n, where):
        return send(
            hid_all.at[pp, tt], hid_all.at[pp, tt], hid_ss.at[n], hid_rs.at[pp, tt], where
        )

    for i, peer in enumerate(z_to):
        copy = hid_send(p, t, i, {"tp": peer})
        copy.start()
        sent.append(copy)

    def scaled(m):
        total = jnp.zeros((rows, col), jnp.float32)
        for tt in range(tp_n):
            h = hid_all[m, tt].astype(jnp.float32)
            total = total + h * h
            xn[m, :, tt * col : (tt + 1) * col] = (h * gain_f[pl.ds(m * tp_n + tt, 1), :]).astype(jnp.bfloat16)
        return total

    def product(m, j, which):
        k_rows = pl.ds(pl.multiple_of(m * pool_w, pool_w), pool_w)
        return jnp.dot(xn[m], slots[j, which, k_rows, :], preferred_element_type=jnp.float32)

    squares = jnp.zeros((rows, col), jnp.float32)
    order = [t] + z_from
    n = tp_n - 1
    for i, tt in enumerate(order):
        if i > 0:
            hid_send(p, tt, i - 1, {"tp": tt}).wait_recv()
        for mate in (p_y, p_c):
            copy = hid_send(p, tt, n, {"pool": mate})
            copy.start()
            sent.append(copy)
            n += 1
        h = hid_all[p, tt].astype(jnp.float32)
        squares = squares + h * h
        x = (h * gain_f[pl.ds(p * tp_n + tt, 1), :]).astype(jnp.bfloat16)
        xn[p, :, pl.ds(pl.multiple_of(tt * col, col), col)] = x
        k_rows = pl.ds(pl.multiple_of((p * tp_n + tt) * col, col), col)

        @pl.loop(0, chunks)
        def _(j, i=i, x=x, k_rows=k_rows):
            if i == 0:
                in_copy(j).wait()
            for which in range(2):
                term = jnp.dot(x, slots[j, which, k_rows, :], preferred_element_type=jnp.float32)
                acc[j, which] = term if i == 0 else acc[j, which] + term

    for tt in order:
        hid_send(p_y, tt, 0, {"pool": p_y}).wait_recv()
        copy = hid_send(p_y, tt, n, {"pool": p_c})
        copy.start()
        sent.append(copy)
        n += 1
    squares = squares + scaled(p_y)
    for tt in order:
        hid_send(p_c, tt, 0, {"pool": p_c}).wait_recv()
    squares = squares + scaled(p_c)
    for tt in order:
        hid_send(p_yc, tt, 0, {"pool": p_c}).wait_recv()
    squares = squares + scaled(p_yc)
    inv = lax.rsqrt(jnp.sum(squares, axis=1, keepdims=True) / (pool_n * pool_w) + 1e-05)
    logits = inv * sum(
        lax.dot_general(
            xn[m],
            router_v[:, m * pool_w : (m + 1) * pool_w],
            NT,
            preferred_element_type=jnp.float32,
        )
        for m in range(pool_n)
    )
    experts = router_v.shape[0]
    own = p // group_size
    lane = lax.broadcasted_iota(jnp.int32, (tokens, experts), 1)
    coeffs = []
    for b in range(batches):
        lb = logits[b * tokens : (b + 1) * tokens]
        id0 = ids_v[b, 0:1, :].reshape(tokens, 1)
        id1 = ids_v[b, 1:2, :].reshape(tokens, 1)
        l0 = jnp.sum(jnp.where(lane == id0, lb, 0.0), axis=1, keepdims=True)
        l1 = jnp.sum(jnp.where(lane == id1, lb, 0.0), axis=1, keepdims=True)
        coeffs.append(
            jnp.where(id0 == own, jax.nn.sigmoid(l0 - l1), 0.0)
            + jnp.where(id1 == own, jax.nn.sigmoid(l1 - l0), 0.0)
        )
    coeff = jnp.concatenate(coeffs, axis=0)

    def gate_up(j):
        gate, up = [
            inv * (acc[j, which] + sum(product(m, j, which) for m in mates)) for which in range(2)
        ]
        act[:, pl.ds(pl.multiple_of(j * CHUNK, CHUNK), CHUNK)] = (
            jax.nn.silu(gate) * up
        ).astype(jnp.bfloat16)

    for j in range(3):
        gate_up(j)
        start_pair(j + 1)

    @pl.loop(3, chunks)
    def _(j):
        gate_up(j)

    def mix_send(n, e, i, peer):
        k = (peer + tp_n - t) % tp_n
        return send(
            mix_s.at[n, e],
            mix_r.at[i, k],
            mix_ss.at[n, e],
            mix_rs.at[i, k],
            {"pool": targets[i], "tp": peer},
        )

    for n, (i, h) in enumerate(groups):
        parts = []
        for c in range(per_half):
            out_copy(n, c).wait()
            parts.append(
                jnp.dot(
                    act[...],
                    slots[places[n // 2], n % 2, c * ffl : (c + 1) * ffl, :],
                    preferred_element_type=jnp.float32,
                )
            )
        whole = jnp.concatenate(parts, axis=1) * coeff
        for e in range(2):
            piece = whole[:, e * col : (e + 1) * col]
            mix_s[n, e] = piece.astype(jnp.bfloat16)
            if n < len(groups) - 1:
                copy = mix_send(n, e, i, 2 * h + e)
                copy.start()
                sent.append(copy)
            else:
                att_rows[:, e * col : (e + 1) * col] = piece
    last = len(groups) - 1
    copy = mix_send(last, 1 - t % 2, pool_n - 1, t + 1 - 2 * (t % 2))
    copy.start()
    sent.append(copy)
    result = hid[...] + piece_of(t % 2)
    for k in range(tp_n):
        for i in range(pool_n):
            if i < pool_n - 1 or k > 0:
                pltpu.make_async_remote_copy(
                    src_ref=mix_r.at[i, k],
                    dst_ref=mix_r.at[i, k],
                    send_sem=mix_ss.at[0, 0],
                    recv_sem=mix_rs.at[i, k],
                    device_id={"pool": targets[i], "tp": (t + tp_n - k) % tp_n},
                    device_id_type=MESH,
                ).wait_recv()
                result = result + mix_r[i, k].astype(jnp.float32)
    for b in range(batches):
        out_ref[b] = result[b * tokens : (b + 1) * tokens].astype(jnp.bfloat16)
    for copy in sent:
        copy.wait_send()


def fused(
    queries,
    new_kv,
    kv_cache,
    cache_lengths,
    residual_in,
    out_weight,
    norm_gain,
    router_weight,
    expert_in,
    expert_out,
    expert_ids,
):
    batches, seqs, q_width = queries.shape
    tokens, col = residual_in.shape[1:]
    rows = batches * tokens
    kvl = new_kv.shape[3] // HD
    group_q = HQ // KVH
    model = norm_gain.shape[0]
    experts = router_weight.shape[1]
    ffl = expert_out.shape[1]
    ctx = kv_cache.shape[3]
    tp_n = 4
    heads = batches * seqs * kvl * 8
    half_w = tp_n * col // 2
    per_half = half_w // CHUNK
    chunks = ffl // CHUNK
    bf, f32 = jnp.bfloat16, jnp.float32
    dma = pltpu.SemaphoreType.DMA
    sizes = (batches, seqs, kvl, group_q, HD, tokens, 4 // experts)
    return pl.pallas_call(
        functools.partial(layer_kernel, sizes),
        out_shape=jax.ShapeDtypeStruct(residual_in.shape, bf),
        in_specs=[pl.BlockSpec(memory_space=pl.ANY)] * 11,
        out_specs=pl.BlockSpec(memory_space=pltpu.VMEM),
        scratch_shapes=[
            pltpu.SMEM((seqs, batches), jnp.int32),
            pltpu.VMEM(queries.shape, bf),
            pltpu.VMEM(new_kv.shape, bf),
            pltpu.VMEM(kv_cache.shape, bf),
            pltpu.VMEM(residual_in.shape, bf),
            pltpu.VMEM((model,), bf),
            pltpu.VMEM((experts, model), bf),
            pltpu.VMEM((batches, 2, tokens), jnp.int32),
            pltpu.VMEM((chunks + 1, 2, model, CHUNK), bf),
            pltpu.VMEM((8, q_width), f32),
            pltpu.VMEM((batches * seqs, 2, kvl * HD), f32),
            pltpu.VMEM((heads, HD), f32),
            pltpu.VMEM((heads, ctx), f32),
            pltpu.VMEM((heads, HD), f32),
            pltpu.VMEM((4, 8, q_width), bf),
            pltpu.VMEM((rows, q_width), f32),
            pltpu.VMEM((tp_n - 1, rows, col), bf),
            pltpu.VMEM((tp_n - 1, rows, col), bf),
            pltpu.VMEM((rows, col), f32),
            pltpu.VMEM((4, tp_n, rows, col), bf),
            pltpu.VMEM((4 * tp_n, col), f32),
            pltpu.VMEM((4, rows, tp_n * col), bf),
            pltpu.VMEM((chunks, 2, rows, CHUNK), f32),
            pltpu.VMEM((rows, ffl), bf),
            pltpu.VMEM((8, 2, rows, col), bf),
            pltpu.VMEM((4, tp_n, rows, col), bf),
            dma((7,)),
            dma,
            dma((tp_n * col // CHUNK,)),
            dma((chunks,)),
            dma((8, per_half)),
            dma((3,)),
            dma((3,)),
            dma((tp_n - 1,)),
            dma((tp_n - 1,)),
            dma((15,)),
            dma((4, tp_n)),
            dma((8, 2)),
            dma((4, tp_n)),
        ],
        compiler_params=pltpu.CompilerParams(
            collective_id=0, has_side_effects=True, vmem_limit_bytes=63 * 1024 * 1024
        ),
        cost_estimate=pl.CostEstimate(
            flops=6 * rows * model * ffl,
            bytes_accessed=6 * model * ffl + 2 * out_weight.size,
            transcendentals=0,
        ),
        name="layer",
    )(
        cache_lengths.T,
        queries,
        new_kv,
        kv_cache,
        residual_in,
        out_weight,
        norm_gain,
        router_weight.T,
        expert_in,
        expert_out,
        expert_ids.transpose(0, 2, 1),
    )


def body(*arrays):
    queries, new_kv, _, _, residual_in, _, norm_gain, router_weight, _, expert_out, _ = arrays
    ffl, model = expert_out.shape[1:]
    col = residual_in.shape[2]
    fits = (
        lax.axis_size("pool") == 4
        and lax.axis_size("tp") == 4
        and 4 % router_weight.shape[1] == 0
        and col % 128 == 0
        and (2 * col) % CHUNK == 0
        and ffl % CHUNK == 0
        and ffl // CHUNK >= 4
        and 4 * col // CHUNK * ffl == 2 * model
        and 4 * col // CHUNK * queries.shape[2] <= 2 * model
        and queries.shape[2] == 4 * col
        and queries.shape[0] * queries.shape[1] <= 8
        and residual_in.shape[1] % 8 == 0
    )
    return fused(*arrays) if fits else shards(*arrays)


def solution(mesh):
    return jax.shard_map(
        body,
        mesh=mesh,
        in_specs=(
            P(None, ("grp", "pool"), "tp"),
            P(None, ("grp", "pool"), None, "tp"),
            P(None, ("grp", "pool"), None, None, "tp"),
            P(None, ("grp", "pool")),
            P(None, "grp", ("pool", "tp")),
            P("tp", "pool"),
            P(),
            P(),
            P("pool", None, None, "tp"),
            P("pool", "tp", None),
            P(None, "grp", None),
        ),
        out_specs=P(None, "grp", ("pool", "tp")),
        check_vma=False,
    )
```
